128 devices in a mesh: slab: 64 (over y, x, z), pencil: 2 (over core).
Axes of the slice: x: 4, y: 4, z: 4, core: 2. Of those that a mesh axis runs over, the one named last changes fastest.
Arguments:
- point_feats: bfloat16 [524288, 64], P(('slab', 'pencil')), may hold values from -6 to 6
- point_x: float32 [524288], P(('slab', 'pencil')), may hold values from 0 to 1
- neighbour_dev: int32 [4096, 4], P(('slab', 'pencil')), may hold values from 0 to 127, all different within a row; in each aligned block of 32 rows (0 to 31, 32 to 63, ...) at most 2 rows name the same one
- neighbour_line: int32 [4096, 4], P(('slab', 'pencil')), may hold values from 0 to 127
- spec_weight: bfloat16 [2, 1024, 32, 2, 64, 64], P(None, ('slab', 'pencil')), may hold values from -4.5 to 4.5
- skip_weight: bfloat16 [2, 64, 64], replicated, may hold values from -0.75 to 0.75
Outputs:
- point_out: float32 [524288, 64], P(('slab', 'pencil'))
The draws below stay inside these ranges and needn't reach their ends.
Inputs may be any that keep to these rules, and one draw needn't show every extreme that they name: `neighbour_dev`: each row names 4 different devices; the rows of one device name any one device at most 2 times, and some device exactly 2 times.
All inputs are finite; a program needn't handle non-finite values.
Results may differ from the reference program's by a relative error of at most 0.003.
Values may be sent and summed in bfloat16 or wider, within the bound.
A program may use at most 192 MiB of HBM per device.

```python
import math
import jax
import jax.numpy as jnp
import numpy as np
from jax import lax

C = 64
G = 128
MODES = 32
PBS = 128
TOP = 4
LAYERS = 2
PB_DEV = 32
ZS = 2
YS = 64
LINES = 128
CAP = 2
PAIRS = 1024
BLOCKS = 4096
POINTS = 524288
N_SLAB = 64
N_PENCIL = 2


def place_ends(array, key, least, largest):
    shape = array.shape
    place = [jax.random.randint(jax.random.fold_in(key, axis), (), 0, shape[axis]) for axis in range(len(shape))]
    array = array.at[tuple(place)].set(least)
    longest = shape.index(max(shape))
    place[longest] = (place[longest] + 1) % shape[longest]
    return array.at[tuple(place)].set(largest)


def level_of(stream_key, extent, split, smallest, largest):
    level = 1.0
    for position, shards_of in split:
        steps = jax.random.uniform(jax.random.fold_in(jax.random.fold_in(stream_key, 6), position), (shards_of,), jnp.float32, smallest / len(split), largest / len(split))
        level = level * jnp.repeat(jnp.exp(steps), extent[position] // shards_of).reshape((-1,) + (1,) * (len(extent) - 1 - position))
    return level


def routed_block(stream_key, own, number, rows, count, top, limit, lean):
    order = jax.random.permutation(stream_key, count)
    heavy_load, usual = portions_of(count, rows * top, limit, lean, True), portions_of(count, rows * top, limit, lean, False)
    places = jnp.arange(count)

    def named(tallies, turn):
        used = int((tallies > 0).sum())
        fixed = max(1, used // 4)
        shifted = fixed + (places - fixed + turn * (used - fixed)) % max(1, count - fixed)
        return jnp.zeros((count,), jnp.int32).at[order[jnp.where(places < fixed, places, shifted)]].set(jnp.asarray(tallies, jnp.int32))

    tallies = jnp.where(number % 4 == 0, named(heavy_load, number // 4), named(usual, number - number // 4 - 1))
    mixed = jax.random.permutation(jax.random.fold_in(own, 3), count)
    donor, receiver = mixed[0:count // 2 * 2:2], mixed[1:count // 2 * 2:2]
    room = jnp.minimum(tallies[donor] - 1, limit - tallies[receiver]) // 2
    room = jnp.where((donor == order[0]) | (receiver == order[0]) | (tallies[receiver] == 0), 0, jnp.maximum(room, 0))
    shifted = jax.random.randint(jax.random.fold_in(own, 4), (count // 2,), 0, 1 << 20) % (room + 1)
    tallies = tallies.at[donor].add(-shifted).at[receiver].add(shifted)
    members = jnp.searchsorted(jnp.cumsum(tallies), jnp.arange(rows * top), side="right").astype(jnp.int32)
    grid = members.reshape(top, rows).T
    grid = grid[jax.random.permutation(jax.random.fold_in(own, 1), rows)]
    turn = jax.random.randint(jax.random.fold_in(own, 2), (rows, 1), 0, top)
    return jnp.take_along_axis(grid, (jnp.arange(top)[None, :] + turn) % top, axis=1)


def portions_of(number_of, total, reach, skew, full):
    portions = [(1 << 20) // math.isqrt(standing ** skew) + 1 for standing in range(1, number_of + 1)]
    largest = reach if full else min(reach, max(-(-total // number_of), total * portions[0] // sum(portions)))
    least = 1 if total - largest >= number_of - 1 else 0
    holding, surplus = [largest] + [least] * (number_of - 1), total - largest - least * (number_of - 1)
    while surplus > 0:
        movable = [i for i in range(1, number_of) if holding[i] < largest] or [i for i in range(1, number_of) if holding[i] < reach]
        mass, budget = sum([portions[i] for i in movable]), surplus
        for i in movable:
            addition = min(reach - holding[i], max(1, budget * portions[i] // mass), surplus)
            holding[i] = holding[i] + addition
            surplus = surplus - addition
    return np.array(holding)


def normal_values(stream_key, dims, spread, most, cuts=(), kind=jnp.bfloat16):
    drawn = spread * jax.random.normal(stream_key, dims, jnp.float32)
    if cuts:
        drawn = drawn * level_of(stream_key, dims, cuts, -0.22, 0.18)
    return jnp.clip(drawn, -most, most).astype(kind)


def setup_inputs(seed: int = 0) -> dict:
    seeds = jax.random.split(jax.random.key(seed), 7)
    point_feats = normal_values(seeds[0], (POINTS, C), 1.0, 6.0, ((0, 128),))
    point_x = jnp.clip(1.0 * jax.random.uniform(seeds[1], (POINTS,), jnp.float32) ** level_of(seeds[1], (POINTS,), ((0, 128),), -0.2, 0.2), 0.0, 1.0)
    neighbour_dev_keys = jax.random.split(jax.random.fold_in(seeds[2], 1), BLOCKS // PB_DEV)
    neighbour_dev_turns = jax.random.permutation(jax.random.fold_in(seeds[2], 3), BLOCKS // PB_DEV)
    neighbour_dev = jax.vmap(lambda own, number: routed_block(jax.random.fold_in(seeds[2], 2), own, number, PB_DEV, N_SLAB * N_PENCIL, TOP, CAP, 2))(neighbour_dev_keys, neighbour_dev_turns).reshape((BLOCKS, TOP))
    neighbour_line = place_ends(jax.random.randint(seeds[3], (BLOCKS, TOP), 0, LINES), jax.random.fold_in(seeds[3], 1), 0, LINES - 1).astype(jnp.int32)
    spec_weight = normal_values(seeds[4], (LAYERS, PAIRS, MODES, 2, C, C), 1.5, 4.5, ((1, 128),))
    skip_weight = normal_values(seeds[5], (LAYERS, C, C), C ** -0.5, 0.75)
    return {"point_feats": point_feats, "point_x": point_x, "neighbour_dev": neighbour_dev, "neighbour_line": neighbour_line, "spec_weight": spec_weight, "skip_weight": skip_weight}


dec_scale = 0.5
spread_cells = 0.5
highest = lax.Precision.HIGHEST


def dft_tables(length, n_modes, grid_len, offset):
    cells = jnp.arange(length, dtype=jnp.int32) + offset
    waves = jnp.arange(n_modes, dtype=jnp.int32) - n_modes // 2
    phase = jnp.mod(cells[:, None] * waves[None, :], grid_len).astype(jnp.float32)
    angle = phase * (2.0 * jnp.pi / grid_len)
    return jnp.cos(angle), jnp.sin(angle)


def kernel_rows(coords, grid_len):
    offset_x = coords[..., None] * grid_len - jnp.arange(grid_len, dtype=jnp.float32)
    return jnp.exp(-offset_x * offset_x / (2.0 * spread_cells * spread_cells)).astype(jnp.bfloat16)


def spectral_layer(field, weight, skip):
    cos_t, sin_t = dft_tables(G, MODES, G, 0)
    x_real = jnp.einsum('zycx,xk->zyck', field, cos_t, precision=highest)
    x_imag = -jnp.einsum('zycx,xk->zyck', field, sin_t, precision=highest)
    y_real = jnp.einsum('zyck,yj->zjkc', x_real, cos_t, precision=highest) + jnp.einsum('zyck,yj->zjkc', x_imag, sin_t, precision=highest)
    y_imag = jnp.einsum('zyck,yj->zjkc', x_imag, cos_t, precision=highest) - jnp.einsum('zyck,yj->zjkc', x_real, sin_t, precision=highest)
    z_real = jnp.einsum('zjkc,zm->mjkc', y_real, cos_t, precision=highest) + jnp.einsum('zjkc,zm->mjkc', y_imag, sin_t, precision=highest)
    z_imag = jnp.einsum('zjkc,zm->mjkc', y_imag, cos_t, precision=highest) - jnp.einsum('zjkc,zm->mjkc', y_real, sin_t, precision=highest)
    z_real = z_real.reshape(MODES, PAIRS, C)
    z_imag = z_imag.reshape(MODES, PAIRS, C)
    w_real = weight[:, :, 0].astype(jnp.float32)
    w_imag = weight[:, :, 1].astype(jnp.float32)
    m_real = jnp.einsum('mqc,qmcd->mqd', z_real, w_real, precision=highest) - jnp.einsum('mqc,qmcd->mqd', z_imag, w_imag, precision=highest)
    m_imag = jnp.einsum('mqc,qmcd->mqd', z_real, w_imag, precision=highest) + jnp.einsum('mqc,qmcd->mqd', z_imag, w_real, precision=highest)
    b_real = jnp.einsum('mqd,zm->zqd', m_real, cos_t, precision=highest) - jnp.einsum('mqd,zm->zqd', m_imag, sin_t, precision=highest)
    b_imag = jnp.einsum('mqd,zm->zqd', m_real, sin_t, precision=highest) + jnp.einsum('mqd,zm->zqd', m_imag, cos_t, precision=highest)
    b_real = b_real.reshape(G, MODES, MODES, C)
    b_imag = b_imag.reshape(G, MODES, MODES, C)
    r_real = jnp.einsum('zjkc,yj->zykc', b_real, cos_t, precision=highest) - jnp.einsum('zjkc,yj->zykc', b_imag, sin_t, precision=highest)
    r_imag = jnp.einsum('zjkc,yj->zykc', b_real, sin_t, precision=highest) + jnp.einsum('zjkc,yj->zykc', b_imag, cos_t, precision=highest)
    spectral = jnp.einsum('zykc,xk->zycx', r_real, cos_t, precision=highest) - jnp.einsum('zykc,xk->zycx', r_imag, sin_t, precision=highest)
    spectral = spectral / float(G * G * G)
    skipped = jnp.einsum('zycx,cd->zydx', field, skip.astype(jnp.float32), precision=highest)
    return jax.nn.gelu(spectral + skipped, approximate=True)


def reference(point_feats, point_x, neighbour_dev, neighbour_line, spec_weight, skip_weight):
    features = point_feats.reshape(BLOCKS, PBS, C).astype(jnp.float32)
    kernel = kernel_rows(point_x.reshape(BLOCKS, PBS), G)
    message = jnp.einsum('bpc,bpx->bcx', features, kernel.astype(jnp.float32)).astype(jnp.bfloat16)
    z_index = (neighbour_dev // N_PENCIL) * ZS + neighbour_line // YS
    y_index = (neighbour_dev % N_PENCIL) * YS + neighbour_line % YS
    global_line = (z_index * G + y_index).astype(jnp.int32)
    grid_lines = jnp.zeros((G * G, C, G), jnp.float32)
    for fan_index in range(TOP):
        grid_lines = grid_lines + jax.ops.segment_sum(message.astype(jnp.float32), global_line[:, fan_index], G * G)
    field = grid_lines.reshape(G, G, C, G)
    for layer_index in range(LAYERS):
        field = spectral_layer(field, spec_weight[layer_index], skip_weight[layer_index])
    grid_out = field.astype(jnp.bfloat16).reshape(G * G, C, G)
    total = jnp.zeros((BLOCKS, PBS, C), jnp.float32)
    for fan_index in range(TOP):
        values = grid_out[global_line[:, fan_index]].astype(jnp.float32)
        pair_term = dec_scale * jnp.einsum('bpx,bcx->bpc', kernel.astype(jnp.float32), values)
        total = total + pair_term
    return total.reshape(POINTS, C)
```

```python
import functools

import jax
import jax.numpy as jnp
import numpy as np
from jax import lax
from jax.experimental import pallas as pl
from jax.experimental.pallas import tpu as pltpu
from jax.sharding import PartitionSpec as P

G = 128
C = 64
M = 32
NDEV = 128
MESH = pl.DeviceIdType.MESH
BF = jnp.bfloat16
F32 = jnp.float32
VLIM = 60 * 1024 * 1024


def trig(cells):
    waves = np.arange(M) - M // 2
    ang = ((cells[:, None] * waves[None, :]) % G) * (2.0 * np.pi / G)
    return np.cos(ang), np.sin(ang)


def split_np(t):
    hi = np.asarray(t, np.float32).astype(jnp.bfloat16)
    lo = (np.asarray(t, np.float64) - hi.astype(np.float64)).astype(np.float32).astype(jnp.bfloat16)
    return hi, lo


def tall(t):
    hi, lo = split_np(t)
    return np.concatenate([np.concatenate([hi, hi], 1), np.concatenate([lo, np.zeros_like(lo)], 1)], 0)


def wide(t):
    hi, lo = split_np(t)
    return np.concatenate([hi, hi, lo], 1)


def make_tables():
    cos, sin = trig(np.arange(G))
    yf = tall(np.concatenate([cos.T, -sin.T], 0))
    zf = []
    for z1 in range(2):
        c, s = trig(2 * np.arange(G // 2) + z1)
        zf.append(tall(np.concatenate([np.concatenate([c.T, s.T], 1), np.concatenate([-s.T, c.T], 1)], 0)))
    zf = np.concatenate(zf, 0)
    xf = tall(np.concatenate([cos.T, sin.T], 0))
    xi = wide(np.concatenate([cos, sin], 1) / float(G) ** 3)
    zi = wide(np.concatenate([np.concatenate(trig(2 * np.arange(G // 2) + z1), 1) for z1 in range(2)], 0))
    yi = wide(np.concatenate([cos, -sin], 1))
    return yf, zf, xf, xi, zi, yi


def split2(v):
    hi = v.astype(BF)
    return hi, (v - hi.astype(F32)).astype(BF)


def dot(a, b):
    return jnp.dot(a, b, preferred_element_type=F32)


def lane_lo(shape):
    return lax.broadcasted_iota(jnp.int32, shape, 1) < C


def swap(v):
    return pltpu.roll(v, C, 1)


def y_forward(yf, plane, a_ref, slab):
    hi, lo = split2(plane)
    out = dot(yf, jnp.concatenate([hi, lo], 0))
    out = out[:2 * M] + out[2 * M:]
    a_ref[pl.ds(slab, M, stride=G), :] = out[:M]
    a_ref[pl.ds(slab + 64, M, stride=G), :] = out[M:]


def z_forward(zf, a_ref, ky):
    hi, lo = split2(a_ref[pl.ds(pl.multiple_of(ky * G, G), G), :])
    out = dot(zf, jnp.concatenate([hi, lo], 0))
    o0 = out[:64] + out[64:128]
    o1 = out[128:192] + out[192:]
    low = lane_lo((M, G))
    main = jnp.where(low, o0[:M], o1[M:])
    other = jnp.where(low, o0[M:], o1[:M])
    return main + swap(other)


def x_forward(xf, plane):
    hi, lo = split2(plane)
    out = dot(xf, jnp.concatenate([hi, lo], 0))
    out = out[:64] + out[64:]
    rot = swap(out[M:])
    return out[:M] + jnp.where(lane_lo((M, G)), rot, -rot)


def stack3(rows):
    hi, lo = split2(rows)
    return jnp.concatenate([hi, lo, hi], 0)


def mode_inverse(table, modes):
    rot = swap(modes)
    rot = jnp.where(lane_lo((M, G)), -rot, rot)
    return dot(table, stack3(jnp.concatenate([modes, rot], 0)))


def z_inverse(zi, modes, iz_ref, ky):
    out = mode_inverse(zi, modes)
    o0, o1 = out[:64], out[64:]
    low = lane_lo((64, G))
    iz_ref[pl.ds(ky, 64, stride=64), :] = jnp.where(low, o0, swap(o1))
    iz_ref[pl.ds(ky + M, 64, stride=64), :] = jnp.where(low, swap(o0), o1)


def gelu(v):
    k = 0.7978845608028654
    return 0.5 * v * (1.0 + jnp.tanh(k * (v + 0.044715 * (v * v * v))))


def y_inverse_act(yi, skip2, iz_ref, plane, slab):
    rows = iz_ref[pl.ds(pl.multiple_of(slab * 64, 64), 64), :]
    hi, lo = split2(plane)
    spectral = dot(yi, stack3(rows))
    skipped = dot(jnp.concatenate([hi, lo], 1), skip2)
    return gelu(spectral + skipped)


def unpack_messages(r_ref, msg_ref):
    def body(sg, _):
        v = r_ref[pl.ds(sg * 8, 8)].reshape(G, G).astype(F32)
        w = swap(v)
        low = lane_lo((G, G))
        msg_ref[sg, :G, :] = jnp.where(low, v, w).astype(BF)
        msg_ref[sg, G:, :] = jnp.where(low, w, v).astype(BF)
        return 0
    lax.fori_loop(0, 16, body, 0)


def expand(msg_ref, ie_ref, rows_ref):
    def body(sg, _):
        idx = ie_ref[sg]
        msg = msg_ref[sg]
        lanes = lax.broadcasted_iota(jnp.int32, (16, 256), 1)
        for og in range(16):
            hot = [jnp.where(idx[:, o:o + 1] == lanes, 1.0, 0.0).astype(BF) for o in range(og * 8, og * 8 + 8)]
            out = dot(jnp.concatenate(hot, 0), msg).astype(BF)
            rows_ref[og * 8:og * 8 + 8, pl.ds(pl.multiple_of(sg * 16, 16), 16), :] = out.reshape(8, 16, G)
        return 0
    lax.fori_loop(0, 16, body, 0)


def scatter_lines(rows_ref, lt_ref, o):
    lines = lax.broadcasted_iota(jnp.int32, (G, 256), 0)
    hot = jnp.where(lt_ref[o] == lines, 1.0, 0.0).astype(BF)
    out = dot(hot, rows_ref[o])
    return jnp.where(lane_lo((64, G)), out[:64], out[64:])


def gather_lines(half, ls, j):
    low = lane_lo((64, G))
    rhs = jnp.concatenate([jnp.where(low, half, 0.0), jnp.where(low, 0.0, half)], 0).astype(BF)
    lanes = lax.broadcasted_iota(jnp.int32, (256, G), 1)
    hot = jnp.where(ls[:, j:j + 1] == lanes, 1.0, 0.0).astype(BF)
    return dot(hot, rhs).astype(BF)


def block_sums(rows2_ref, iet_ref, out_ref):
    def body(sg, _):
        codes = iet_ref[sg]
        rows = lax.broadcasted_iota(jnp.int32, (256, 256), 0)
        acc = jnp.zeros((256, G), F32)
        for k in range(8):
            hot = jnp.where(codes[:, k * 256:(k + 1) * 256] == rows, 1.0, 0.0).astype(BF)
            acc = acc + dot(hot, rows2_ref[sg, k * 16:(k + 1) * 16].reshape(256, G))
        acc = acc + swap(acc)
        out = jnp.where(lane_lo((G, G)), acc[:G], acc[G:]).astype(BF)
        out_ref[pl.ds(sg * 8, 8)] = out.reshape(8, 16, G)
        return 0
    lax.fori_loop(0, 16, body, 0)


def mode_product(f8, w_ref, kz):
    low = lane_lo((8, G))
    a = jnp.where(low, f8, -f8)
    b = swap(f8)
    ah, al = split2(a)
    bh, bl = split2(b)
    lhs = jnp.concatenate([ah.astype(F32), al.astype(F32), bh.astype(F32), bl.astype(F32)], 0).astype(BF)
    row = lax.broadcasted_iota(jnp.int32, (8, C), 0)
    re = jnp.zeros((8, C), F32)
    im = jnp.zeros((8, C), F32)
    for j in range(8):
        out = dot(lhs, w_ref[j, kz])
        re = jnp.where(row == j, out[0:8] + out[8:16], re)
        im = jnp.where(row == j, out[16:24] + out[24:32], im)
    return jnp.concatenate([re, im], 1)


def encode_kernel(r_ref, ie_ref, lt_ref, yf_ref, zf_ref, field_ref, send_ref, msg_ref, rows_ref, a_ref):
    unpack_messages(r_ref, msg_ref)
    expand(msg_ref, ie_ref, rows_ref)

    def per_slab(slab, _):
        plane = jnp.concatenate([scatter_lines(rows_ref, lt_ref, 2 * slab), scatter_lines(rows_ref, lt_ref, 2 * slab + 1)], 0)
        field_ref[slab] = plane
        y_forward(yf_ref[...], plane, a_ref, slab)
        return 0
    lax.fori_loop(0, 64, per_slab, 0)
    forward_modes(zf_ref, a_ref, send_ref)


def forward_modes(zf_ref, a_ref, send_ref):
    def per_ky(ky, _):
        send_ref[pl.ds(ky * 4, 4)] = z_forward(zf_ref[...], a_ref, ky).reshape(4, 8, G)
        return 0
    lax.fori_loop(0, M, per_ky, 0)


def inverse_modes(rx_ref, zi_ref, iz_ref):
    def per_ky(ky, _):
        z_inverse(zi_ref[...], rx_ref[pl.ds(ky * 4, 4)].reshape(M, G), iz_ref, ky)
        return 0
    lax.fori_loop(0, M, per_ky, 0)


def middle_kernel(rx_ref, field_ref, skip2_ref, zi_ref, yi_ref, yf_ref, zf_ref, out_ref, send_ref, iz_ref, a_ref):
    inverse_modes(rx_ref, zi_ref, iz_ref)

    def per_slab(slab, _):
        plane = y_inverse_act(yi_ref[...], skip2_ref[...], iz_ref, field_ref[slab], slab)
        out_ref[slab] = plane
        y_forward(yf_ref[...], plane, a_ref, slab)
        return 0
    lax.fori_loop(0, 64, per_slab, 0)
    forward_modes(zf_ref, a_ref, send_ref)


def final_kernel(rx_ref, field_ref, skip2_ref, zi_ref, yi_ref, ls_ref, iet_ref, out_ref, iz_ref, rows2_ref):
    inverse_modes(rx_ref, zi_ref, iz_ref)

    def per_group(g, _):
        ls = ls_ref[g]
        for i in range(4):
            slab = g * 4 + i
            plane = y_inverse_act(yi_ref[...], skip2_ref[...], iz_ref, field_ref[slab], slab)
            for p in range(2):
                got = gather_lines(plane[64 * p:64 * p + 64], ls, 2 * i + p)
                rows2_ref[:, 2 * slab + p, :, :] = got.reshape(16, 16, G)
        return 0
    lax.fori_loop(0, 16, per_group, 0)
    block_sums(rows2_ref, iet_ref, out_ref)


def spectrum_kernel(rx_ref, w_ref, xf_ref, xi_ref, out_ref, gs_ref, gr_ref, hs_ref, hr_ref, sems):
    slab = lax.axis_index("slab")
    pencil = lax.axis_index("pencil")
    q = lax.rem(slab, 2) * 2 + pencil
    base = slab - lax.rem(slab, 2)

    def peer(i):
        other = lax.rem(q + i, 4)
        return other, (base + lax.div(other, 2), lax.rem(other, 2))

    barrier = pltpu.get_barrier_semaphore()
    for i in range(1, 4):
        pl.semaphore_signal(barrier, inc=1, device_id=peer(i)[1], device_id_type=MESH)

    rows = rx_ref.shape[0]

    def fwd(kz, _):
        plane = rx_ref[pl.ds(kz, G, stride=8), :]
        gs_ref[:, kz] = x_forward(xf_ref[...], plane).reshape(4, 8, G)
        return 0
    lax.fori_loop(0, 8, fwd, 0)

    def exchange(src, dst, st):
        local = pltpu.make_async_copy(src.at[q], dst.at[q], sems.at[st, 2])
        local.start()
        if st == 0:
            pl.semaphore_wait(barrier, 3)
        for i in range(1, 4):
            other, did = peer(i)
            pltpu.make_async_remote_copy(src.at[other], dst.at[q], sems.at[st, 0], sems.at[st, 1], device_id=did, device_id_type=MESH).start()
        local.wait()
        three = pl.ds(0, 3)
        pltpu.make_async_copy(src.at[three], src.at[three], sems.at[st, 0]).wait()
        pltpu.make_async_copy(dst.at[three], dst.at[three], sems.at[st, 1]).wait()

    exchange(gs_ref, gr_ref, 0)

    def modes(kz, _):
        g, k = lax.div(kz, 8), lax.rem(kz, 8)
        hs_ref[g, k] = mode_product(gr_ref[g, k], w_ref, kz)
        return 0
    lax.fori_loop(0, M, modes, 0)
    exchange(hs_ref, hr_ref, 1)

    def inv(kz, _):
        out_ref[pl.ds(kz, G, stride=8), :] = mode_inverse(xi_ref[...], hr_ref[:, kz].reshape(M, G))
        return 0
    lax.fori_loop(0, 8, inv, 0)


def call(kernel, outs, args, scratch, name, **params):
    vm = pl.BlockSpec(memory_space=pltpu.VMEM)
    return pl.pallas_call(
        kernel,
        out_shape=[jax.ShapeDtypeStruct(s, d) for s, d in outs],
        in_specs=[vm] * len(args),
        out_specs=[vm] * len(outs),
        scratch_shapes=scratch,
        compiler_params=pltpu.CompilerParams(vmem_limit_bytes=VLIM, **params),
        name=name,
    )(*args)


def kernel_rows(coords):
    offset_x = coords[..., None] * G - jnp.arange(G, dtype=F32)
    return jnp.exp(-offset_x * offset_x / (2.0 * 0.5 * 0.5)).astype(BF)


def slot_tables(neighbour_dev, neighbour_line):
    nb, fan = neighbour_dev.shape
    dev = neighbour_dev.reshape(-1)
    code = (jnp.arange(nb * fan, dtype=jnp.int32) // fan) * G + neighbour_line.reshape(-1)
    hit = dev[:, None] == jnp.arange(NDEV, dtype=jnp.int32)[None, :]
    first = jnp.min(jnp.where(hit, code[:, None], nb * G), axis=0)
    last = jnp.max(jnp.where(hit, code[:, None], -1), axis=0)
    first = jnp.where(first == nb * G, -1, first)
    second = jnp.where(last == first, -1, last)
    return jnp.stack([first, second], 0)


def route_tables(codes):
    s8 = (jnp.arange(NDEV, dtype=jnp.int32) % 8)[:, None, None]
    block = codes // G
    kpos = jnp.where(codes >= 0, (block // 16) * 128 + s8 * 16 + block % 16, -1)
    line = jnp.where(codes >= 0, codes % G, -1)
    ie = kpos.reshape(16, 16, NDEV)
    iet = ie.transpose(0, 2, 1).reshape(16, 1, 2048)
    flat = line.reshape(256, NDEV)
    lt = flat.T.reshape(NDEV, 1, 256)
    ls = flat.reshape(256, 16, 8).transpose(1, 0, 2)
    return ie, iet, lt, ls


def all_to_all(v):
    return lax.all_to_all(v, ("slab", "pencil"), split_axis=0, concat_axis=0, tiled=True)


def per_device(point_feats, point_x, neighbour_dev, neighbour_line, spec_weight, skip_weight):
    yf, zf, xf, xi, zi, yi = [jnp.asarray(t) for t in make_tables()]
    nb = neighbour_dev.shape[0]
    feats = point_feats.reshape(nb, -1, C)
    kernel = kernel_rows(point_x.reshape(nb, -1))
    codes = lax.all_gather(slot_tables(neighbour_dev, neighbour_line), ("slab", "pencil"), axis=0)
    message = jnp.einsum("bpx,bpc->bxc", kernel, feats, preferred_element_type=F32).astype(BF)
    outgoing = message.reshape(2, 16, G, C).transpose(2, 1, 0, 3).reshape(G, 16, 2 * C)
    arrived = all_to_all(outgoing)
    ie, iet, lt, ls = route_tables(codes)
    zero = jnp.zeros((C, C), BF)
    sk = [jnp.block([[w, zero], [zero, w]]) for w in skip_weight]
    skip2 = [jnp.concatenate([s, s], 0) for s in sk]
    weights = spec_weight.reshape(2, 8, M, 2 * C, C)

    mode_shape = ((NDEV, 8, G), F32)
    field_shape = ((64, G, G), F32)
    field, send = call(
        encode_kernel, [field_shape, mode_shape], [arrived, ie, lt, yf, zf],
        [pltpu.VMEM((16, 256, G), BF), pltpu.VMEM((NDEV, 256, G), BF), pltpu.VMEM((M * G, G), F32)], "encode",
    )

    def spectrum(send, layer):
        rx = all_to_all(send).reshape(NDEV * 8, G)
        (back,) = call(
            spectrum_kernel, [((NDEV * 8, G), F32)], [rx, weights[layer], xf, xi],
            [pltpu.VMEM((4, 8, 8, G), F32)] * 4 + [pltpu.SemaphoreType.DMA((2, 3))], f"spectrum{layer}",
            collective_id=1 + layer, has_side_effects=True,
        )
        return all_to_all(back.reshape(NDEV, 8, G))

    back = spectrum(send, 0)
    field, send = call(
        middle_kernel, [field_shape, mode_shape], [back, field, skip2[0], zi, yi, yf, zf],
        [pltpu.VMEM((64 * 64, G), F32), pltpu.VMEM((M * G, G), F32)], "middle",
    )
    back = spectrum(send, 1)
    (sums,) = call(
        final_kernel, [((NDEV, 16, G), BF)], [back, field, skip2[1], zi, yi, ls, iet],
        [pltpu.VMEM((64 * 64, G), F32), pltpu.VMEM((16, NDEV, 16, G), BF)], "final",
    )
    values = all_to_all(sums)
    values = values.reshape(G, 16, 2, C).transpose(2, 1, 0, 3).reshape(nb, G, C)
    out = 0.5 * jnp.einsum("bpx,bxc->bpc", kernel, values, preferred_element_type=F32)
    return out.reshape(-1, C)


def solution(mesh):
    both = ("slab", "pencil")
    in_specs = (P(both, None), P(both), P(both, None), P(both, None), P(None, both, None, None, None, None), P())
    return jax.shard_map(per_device, mesh=mesh, in_specs=in_specs, out_specs=P(both, None), check_vma=False)
```

```python
import functools

import jax
import jax.numpy as jnp
import numpy as np
from jax import lax
from jax.experimental import pallas as pl
from jax.experimental.pallas import tpu as pltpu
from jax.sharding import PartitionSpec as P

G = 128
C = 64
M = 32
NDEV = 128
MESH = pl.DeviceIdType.MESH
BF = jnp.bfloat16
F32 = jnp.float32
VLIM = 60 * 1024 * 1024


def trig(cells):
    waves = np.arange(M) - M // 2
    ang = ((cells[:, None] * waves[None, :]) % G) * (2.0 * np.pi / G)
    return np.cos(ang), np.sin(ang)


def split_np(t):
    hi = np.asarray(t, np.float32).astype(jnp.bfloat16)
    lo = (np.asarray(t, np.float64) - hi.astype(np.float64)).astype(np.float32).astype(jnp.bfloat16)
    return hi, lo


def tall(t):
    hi, lo = split_np(t)
    return np.concatenate([np.concatenate([hi, hi], 1), np.concatenate([lo, np.zeros_like(lo)], 1)], 0)


def wide(t):
    hi, lo = split_np(t)
    return np.concatenate([hi, hi, lo], 1)


def make_tables():
    cos, sin = trig(np.arange(G))
    yf = tall(np.concatenate([cos.T, -sin.T], 0))
    zf = []
    for z1 in range(2):
        c, s = trig(2 * np.arange(G // 2) + z1)
        zf.append(tall(np.concatenate([np.concatenate([c.T, s.T], 1), np.concatenate([-s.T, c.T], 1)], 0)))
    zf = np.concatenate(zf, 0)
    xf = tall(np.concatenate([cos.T, sin.T], 0))
    xi = wide(np.concatenate([cos, sin], 1) / float(G) ** 3)
    zi = wide(np.concatenate([np.concatenate(trig(2 * np.arange(G // 2) + z1), 1) for z1 in range(2)], 0))
    yi = wide(np.concatenate([cos, -sin], 1))
    return yf, zf, xf, xi, zi, yi


def split2(v):
    hi = v.astype(BF)
    return hi, (v - hi.astype(F32)).astype(BF)


def dot(a, b):
    return jnp.dot(a, b, preferred_element_type=F32)


def lane_lo(shape):
    return lax.broadcasted_iota(jnp.int32, shape, 1) < C


def swap(v):
    return pltpu.roll(v, C, 1)


def y_forward(yf, plane, a_ref, slab):
    hi, lo = split2(plane)
    out = dot(yf, jnp.concatenate([hi, lo], 0))
    out = out[:2 * M] + out[2 * M:]
    a_ref[pl.ds(slab, M, stride=G), :] = out[:M]
    a_ref[pl.ds(slab + 64, M, stride=G), :] = out[M:]


def z_forward(zf, a_ref, ky):
    hi, lo = split2(a_ref[pl.ds(pl.multiple_of(ky * G, G), G), :])
    out = dot(zf, jnp.concatenate([hi, lo], 0))
    o0 = out[:64] + out[64:128]
    o1 = out[128:192] + out[192:]
    low = lane_lo((M, G))
    main = jnp.where(low, o0[:M], o1[M:])
    other = jnp.where(low, o0[M:], o1[:M])
    return main + swap(other)


def x_forward(xf, plane):
    hi, lo = split2(plane)
    out = dot(xf, jnp.concatenate([hi, lo], 0))
    out = out[:64] + out[64:]
    rot = swap(out[M:])
    return out[:M] + jnp.where(lane_lo((M, G)), rot, -rot)


def stack3(rows):
    hi, lo = split2(rows)
    return jnp.concatenate([hi, lo, hi], 0)


def mode_inverse(table, modes):
    rot = swap(modes)
    rot = jnp.where(lane_lo((M, G)), -rot, rot)
    return dot(table, stack3(jnp.concatenate([modes, rot], 0)))


def z_inverse(zi, modes, iz_ref, ky):
    out = mode_inverse(zi, modes)
    o0, o1 = out[:64], out[64:]
    low = lane_lo((64, G))
    iz_ref[pl.ds(ky, 64, stride=64), :] = jnp.where(low, o0, swap(o1))
    iz_ref[pl.ds(ky + M, 64, stride=64), :] = jnp.where(low, swap(o0), o1)


def gelu(v):
    k = 0.7978845608028654
    return 0.5 * v * (1.0 + jnp.tanh(k * (v + 0.044715 * (v * v * v))))


def y_inverse_act(yi, skip2, iz_ref, plane, slab):
    rows = iz_ref[pl.ds(pl.multiple_of(slab * 64, 64), 64), :]
    hi, lo = split2(plane)
    spectral = dot(yi, stack3(rows))
    skipped = dot(jnp.concatenate([hi, lo], 1), skip2)
    return gelu(spectral + skipped)


def unpack_messages(r_ref, msg_ref):
    def body(sg, _):
        v = r_ref[pl.ds(sg * 8, 8)].reshape(G, G).astype(F32)
        w = swap(v)
        low = lane_lo((G, G))
        msg_ref[sg, :G, :] = jnp.where(low, v, w).astype(BF)
        msg_ref[sg, G:, :] = jnp.where(low, w, v).astype(BF)
        return 0
    lax.fori_loop(0, 16, body, 0)


def expand(msg_ref, ie_ref, rows_ref):
    def body(sg, _):
        idx = ie_ref[sg]
        msg = msg_ref[sg]
        lanes = lax.broadcasted_iota(jnp.int32, (16, 256), 1)
        for og in range(16):
            hot = [jnp.where(idx[:, o:o + 1] == lanes, 1.0, 0.0).astype(BF) for o in range(og * 8, og * 8 + 8)]
            out = dot(jnp.concatenate(hot, 0), msg).astype(BF)
            rows_ref[og * 8:og * 8 + 8, pl.ds(pl.multiple_of(sg * 16, 16), 16), :] = out.reshape(8, 16, G)
        return 0
    lax.fori_loop(0, 16, body, 0)


def scatter_lines(rows_ref, lt_ref, o):
    lines = lax.broadcasted_iota(jnp.int32, (G, 256), 0)
    hot = jnp.where(lt_ref[o] == lines, 1.0, 0.0).astype(BF)
    out = dot(hot, rows_ref[o])
    return jnp.where(lane_lo((64, G)), out[:64], out[64:])


def gather_lines(half, ls, j):
    low = lane_lo((64, G))
    rhs = jnp.concatenate([jnp.where(low, half, 0.0), jnp.where(low, 0.0, half)], 0).astype(BF)
    lanes = lax.broadcasted_iota(jnp.int32, (256, G), 1)
    hot = jnp.where(ls[:, j:j + 1] == lanes, 1.0, 0.0).astype(BF)
    return dot(hot, rhs)


def block_sums(rows2_ref, ie_ref, out_ref):
    def body(sg, _):
        codes = ie_ref[sg]
        rows = lax.broadcasted_iota(jnp.int32, (256, G), 0)
        acc = jnp.zeros((256, G), F32)
        for k in range(8):
            hot = [jnp.where(codes[i:i + 1, :] == rows, 1.0, 0.0).astype(BF) for i in (2 * k, 2 * k + 1)]
            part = rows2_ref[pl.ds(pl.multiple_of(sg * 2048 + k * 256, 256), 256), :].astype(BF)
            acc = acc + dot(jnp.concatenate(hot, 1), part)
        acc = acc + swap(acc)
        out = jnp.where(lane_lo((G, G)), acc[:G], acc[G:]).astype(BF)
        out_ref[pl.ds(sg * 8, 8)] = out.reshape(8, 16, G)
        return 0
    lax.fori_loop(0, 16, body, 0)


def mode_product(f8, w_ref, kz):
    low = lane_lo((8, G))
    a = jnp.where(low, f8, -f8)
    b = swap(f8)
    ah, al = split2(a)
    bh, bl = split2(b)
    lhs = jnp.concatenate([ah.astype(F32), al.astype(F32), bh.astype(F32), bl.astype(F32)], 0).astype(BF)
    row = lax.broadcasted_iota(jnp.int32, (8, C), 0)
    re = jnp.zeros((8, C), F32)
    im = jnp.zeros((8, C), F32)
    for j in range(8):
        out = dot(lhs, w_ref[j, kz])
        re = jnp.where(row == j, out[0:8] + out[8:16], re)
        im = jnp.where(row == j, out[16:24] + out[24:32], im)
    return jnp.concatenate([re, im], 1)


def forward_modes(zf_ref, a_ref, send_ref):
    def per_ky(ky, _):
        send_ref[pl.ds(ky * 4, 4)] = z_forward(zf_ref[...], a_ref, ky).reshape(4, 8, G)
        return 0
    lax.fori_loop(0, M, per_ky, 0)


def inverse_modes(rx_ref, zi_ref, iz_ref):
    def per_ky(ky, _):
        z_inverse(zi_ref[...], rx_ref[pl.ds(ky * 4, 4)].reshape(M, G), iz_ref, ky)
        return 0
    lax.fori_loop(0, M, per_ky, 0)


def net_kernel(msg_in, codes_in, w_hbm, skip2_ref, yf_ref, zf_ref, xf_ref, xi_ref, zi_ref, yi_ref, out_ref,
               recv_ref, codes_ref, send_ref, rx_ref, back_ref, sums_ref, gs_ref, gr_ref, hs_ref, hr_ref,
               w_ref, msg_ref, ie_ref, line_ref, lt_ref, rows_ref, rows2_ref, field_ref, a_ref, iz_ref,
               sems, group_sems, w_sems):
    slab = lax.axis_index("slab")
    pencil = lax.axis_index("pencil")
    me = slab * 2 + pencil
    q = lax.rem(slab, 2) * 2 + pencil
    base = slab - lax.rem(slab, 2)

    def partner(i):
        d = lax.rem(me + i, NDEV)
        return d, (lax.div(d, 2), lax.rem(d, 2))

    def peer(i):
        other = lax.rem(q + i, 4)
        return other, (base + lax.div(other, 2), lax.rem(other, 2))

    barrier = pltpu.get_barrier_semaphore()

    def greet(i, _):
        pl.semaphore_signal(barrier, inc=1, device_id=partner(i)[1], device_id_type=MESH)
        return 0
    lax.fori_loop(1, NDEV, greet, 0)
    loads = [pltpu.make_async_copy(w_hbm.at[l], w_ref.at[l], w_sems.at[l]) for l in range(2)]
    for load in loads:
        load.start()
    pl.semaphore_wait(barrier, NDEV - 1)

    def local(src, dst, st):
        return pltpu.make_async_copy(src.at[me] if src.shape[0] == NDEV else src, dst.at[me], sems.at[st, 2])

    def send_all(src, dst, st):
        local(src, dst, st).start()

        def one(i, _):
            d, did = partner(i)
            part = src.at[d] if src.shape[0] == NDEV else src
            pltpu.make_async_remote_copy(part, dst.at[me], sems.at[st, 0], sems.at[st, 1], device_id=did, device_id_type=MESH).start()
            return 0
        lax.fori_loop(1, NDEV, one, 0)

    def wait_all(src, dst, st):
        local(src, dst, st).wait()
        rest = dst.at[pl.ds(0, NDEV - 1)]
        pltpu.make_async_copy(rest, rest, sems.at[st, 0]).wait()
        pltpu.make_async_copy(rest, rest, sems.at[st, 1]).wait()

    def exchange(src, dst, st):
        own = pltpu.make_async_copy(src.at[q], dst.at[q], group_sems.at[st, 2])
        own.start()
        for i in range(1, 4):
            other, did = peer(i)
            pltpu.make_async_remote_copy(src.at[other], dst.at[q], group_sems.at[st, 0], group_sems.at[st, 1],
                                         device_id=did, device_id_type=MESH).start()
        own.wait()
        three = pl.ds(0, 3)
        pltpu.make_async_copy(src.at[three], src.at[three], group_sems.at[st, 0]).wait()
        pltpu.make_async_copy(dst.at[three], dst.at[three], group_sems.at[st, 1]).wait()

    send_all(codes_in, codes_ref, 0)
    send_all(msg_in, recv_ref, 1)
    wait_all(codes_in, codes_ref, 0)
    codes = codes_ref[...].reshape(256, G)
    s8 = lax.rem(lax.div(lax.broadcasted_iota(jnp.int32, (256, G), 0), 2), 8)
    block = lax.shift_right_arithmetic(codes, 7)
    kpos = lax.shift_left(lax.shift_right_arithmetic(block, 4), 7) + s8 * 16 + (block & 15)
    line = jnp.where(codes >= 0, codes & 127, -1)
    ie_ref[...] = jnp.where(codes >= 0, kpos, -1).reshape(16, 16, G)
    line_ref[...] = line
    lt_ref[...] = line.T.reshape(NDEV, 1, 256)
    wait_all(msg_in, recv_ref, 1)

    unpack_messages(recv_ref, msg_ref)
    expand(msg_ref, ie_ref, rows_ref)

    def first(s, _):
        plane = jnp.concatenate([scatter_lines(rows_ref, lt_ref, 2 * s), scatter_lines(rows_ref, lt_ref, 2 * s + 1)], 0)
        field_ref[s] = plane
        y_forward(yf_ref[...], plane, a_ref, s)
        return 0
    lax.fori_loop(0, 64, first, 0)

    for layer in range(2):
        st = 2 + 2 * layer
        forward_modes(zf_ref, a_ref, send_ref)
        rx = rx_ref.at[layer]
        send_all(send_ref, rx, st)
        wait_all(send_ref, rx, st)
        gs, gr, hs, hr = gs_ref, gr_ref.at[layer], hs_ref, hr_ref.at[layer]

        def fwd(kz, _):
            plane = rx.reshape(NDEV * 8, G)[pl.ds(kz, G, stride=8), :]
            gs[:, kz] = x_forward(xf_ref[...], plane).reshape(4, 8, G)
            return 0
        lax.fori_loop(0, 8, fwd, 0)
        exchange(gs, gr, 2 * layer)
        loads[layer].wait()

        def modes(kz, _):
            g, k = lax.div(kz, 8), lax.rem(kz, 8)
            hs[g, k] = mode_product(gr[g, k], w_ref.at[layer], kz)
            return 0
        lax.fori_loop(0, M, modes, 0)
        exchange(hs, hr, 2 * layer + 1)

        def inv(kz, _):
            send_ref.reshape(NDEV * 8, G)[pl.ds(kz, G, stride=8), :] = mode_inverse(xi_ref[...], hr[:, kz].reshape(M, G))
            return 0
        lax.fori_loop(0, 8, inv, 0)
        back = back_ref.at[layer]
        send_all(send_ref, back, st + 1)
        wait_all(send_ref, back, st + 1)
        inverse_modes(back, zi_ref, iz_ref)
        if layer == 0:
            def middle(s, _):
                plane = y_inverse_act(yi_ref[...], skip2_ref[0], iz_ref, field_ref[s], s)
                field_ref[s] = plane
                y_forward(yf_ref[...], plane, a_ref, s)
                return 0
            lax.fori_loop(0, 64, middle, 0)
        else:
            def final(g, _):
                ls = pltpu.roll(line_ref[...], lax.rem(NDEV - 8 * g, NDEV), 1)
                for i in range(4):
                    s = g * 4 + i
                    plane = y_inverse_act(yi_ref[...], skip2_ref[1], iz_ref, field_ref[s], s)
                    for p in range(2):
                        rows2_ref[pl.ds(2 * s + p, 256, stride=G), :] = gather_lines(plane[64 * p:64 * p + 64], ls, 2 * i + p)
                return 0
            lax.fori_loop(0, 16, final, 0)

    block_sums(rows2_ref, ie_ref, sums_ref)
    send_all(sums_ref, out_ref, 6)
    wait_all(sums_ref, out_ref, 6)


def kernel_rows(coords):
    offset_x = coords[..., None] * G - jnp.arange(G, dtype=F32)
    return jnp.exp(-offset_x * offset_x / (2.0 * 0.5 * 0.5)).astype(BF)


def slot_tables(neighbour_dev, neighbour_line):
    nb, fan = neighbour_dev.shape
    dev = neighbour_dev.reshape(-1)
    code = (jnp.arange(nb * fan, dtype=jnp.int32) // fan) * G + neighbour_line.reshape(-1)
    hit = dev[:, None] == jnp.arange(NDEV, dtype=jnp.int32)[None, :]
    first = jnp.min(jnp.where(hit, code[:, None], nb * G), axis=0)
    last = jnp.max(jnp.where(hit, code[:, None], -1), axis=0)
    first = jnp.where(first == nb * G, -1, first)
    second = jnp.where(last == first, -1, last)
    return jnp.stack([first, second], 0)


def per_device(point_feats, point_x, neighbour_dev, neighbour_line, spec_weight, skip_weight):
    yf, zf, xf, xi, zi, yi = [jnp.asarray(t) for t in make_tables()]
    nb = neighbour_dev.shape[0]
    feats = point_feats.reshape(nb, -1, C)
    kernel = kernel_rows(point_x.reshape(nb, -1))
    codes = slot_tables(neighbour_dev, neighbour_line)
    message = jnp.einsum("bpx,bpc->bxc", kernel, feats, preferred_element_type=F32).astype(BF)
    outgoing = message.reshape(2, 16, G, C).transpose(2, 1, 0, 3).reshape(G, 16, 2 * C)
    zero = jnp.zeros((C, C), BF)
    skip2 = jnp.stack([jnp.concatenate([jnp.block([[w, zero], [zero, w]])] * 2, 0) for w in skip_weight])
    weights = spec_weight.reshape(2, 8, M, 2 * C, C)
    vm = pl.BlockSpec(memory_space=pltpu.VMEM)
    modes = pltpu.VMEM((NDEV, 8, G), F32)
    pair = pltpu.VMEM((2, NDEV, 8, G), F32)
    group = pltpu.VMEM((4, 8, 8, G), F32)
    group2 = pltpu.VMEM((2, 4, 8, 8, G), F32)
    values = pl.pallas_call(
        net_kernel,
        out_shape=jax.ShapeDtypeStruct((NDEV, 16, G), BF),
        in_specs=[vm, vm, pl.BlockSpec(memory_space=pl.ANY)] + [vm] * 7,
        out_specs=vm,
        scratch_shapes=[
            pltpu.VMEM((NDEV, 16, G), BF), pltpu.VMEM((NDEV, 2, G), jnp.int32), modes, pair, pair, pltpu.VMEM((NDEV, 16, G), BF),
            group, group2, group, group2,
            pltpu.VMEM((2, 8, M, 2 * C, C), BF), pltpu.VMEM((16, 256, G), BF), pltpu.VMEM((16, 16, G), jnp.int32),
            pltpu.VMEM((256, G), jnp.int32), pltpu.VMEM((NDEV, 1, 256), jnp.int32), pltpu.VMEM((NDEV, 256, G), BF),
            pltpu.VMEM((256 * G, G), F32), pltpu.VMEM((64, G, G), F32), pltpu.VMEM((M * G, G), F32), pltpu.VMEM((64 * 64, G), F32),
            pltpu.SemaphoreType.DMA((7, 3)), pltpu.SemaphoreType.DMA((4, 3)), pltpu.SemaphoreType.DMA((2,)),
        ],
        compiler_params=pltpu.CompilerParams(vmem_limit_bytes=VLIM, collective_id=1, has_side_effects=True),
        name="net",
    )(outgoing, codes, weights, skip2, yf, zf, xf, xi, zi, yi)
    values = values.reshape(G, 16, 2, C).transpose(2, 1, 0, 3).reshape(nb, G, C)
    out = 0.5 * jnp.einsum("bpx,bxc->bpc", kernel, values, preferred_element_type=F32)
    return out.reshape(-1, C)


def solution(mesh):
    both = ("slab", "pencil")
    in_specs = (P(both, None), P(both), P(both, None), P(both, None), P(None, both, None, None, None, None), P())
    return jax.shard_map(per_device, mesh=mesh, in_specs=in_specs, out_specs=P(both, None), check_vma=False)
```

```python
import jax
import jax.numpy as jnp
import numpy as np
from jax import lax
from jax.experimental import pallas as pl
from jax.experimental.pallas import tpu as pltpu
from jax.sharding import PartitionSpec as P

G = 128
C = 64
M = 32
NDEV = 128
MESH = pl.DeviceIdType.MESH
BF = jnp.bfloat16
F32 = jnp.float32
VLIM = 60 * 1024 * 1024


def trig(cells):
    waves = np.arange(M) - M // 2
    ang = ((cells[:, None] * waves[None, :]) % G) * (2.0 * np.pi / G)
    return np.cos(ang), np.sin(ang)


def split_np(t):
    hi = np.asarray(t, np.float32).astype(jnp.bfloat16)
    lo = (np.asarray(t, np.float64) - hi.astype(np.float64)).astype(np.float32).astype(jnp.bfloat16)
    return hi, lo


def tall(t):
    hi, lo = split_np(t)
    return np.concatenate([np.concatenate([hi, hi], 1), np.concatenate([lo, np.zeros_like(lo)], 1)], 0)


def wide(t):
    hi, lo = split_np(t)
    return np.concatenate([hi, hi, lo], 1)


def make_tables():
    cos, sin = trig(np.arange(G))
    yf = tall(np.concatenate([cos.T, -sin.T], 0))
    zf = []
    for z1 in range(2):
        c, s = trig(2 * np.arange(G // 2) + z1)
        zf.append(tall(np.concatenate([np.concatenate([c.T, s.T], 1), np.concatenate([-s.T, c.T], 1)], 0)))
    zf = np.concatenate(zf, 0)
    xf = tall(np.concatenate([cos.T, sin.T], 0))
    xi = wide(np.concatenate([cos, sin], 1) / float(G) ** 3)
    zi = wide(np.concatenate([np.concatenate(trig(2 * np.arange(G // 2) + z1), 1) for z1 in range(2)], 0))
    yi = wide(np.concatenate([cos, -sin], 1))
    return yf, zf, xf, xi, zi, yi


ROWS_STRIDE = 72
A_STRIDE = 136
IZ_STRIDE = 72
MSG_STRIDE = 24
cat = jnp.concatenate


def split2(v):
    hi = v.astype(BF)
    return hi, (v - hi.astype(F32)).astype(BF)


def dot(a, b):
    return jnp.dot(a, b, preferred_element_type=F32)


def tdot(a, b):
    return lax.dot_general(a, b, (((0,), (0,)), ((), ())), preferred_element_type=F32)


def lane_lo(shape):
    return lax.broadcasted_iota(jnp.int32, shape, 1) < C


def swap(v):
    return pltpu.roll(v, C, 1)


def lanes(v, n):
    return [v[:, i * G:(i + 1) * G] for i in range(n)]


def stack2(planes):
    parts = [split2(p) for p in planes]
    return cat([cat([h for h, _ in parts], 1), cat([l for _, l in parts], 1)], 0)


def stack3(planes):
    parts = [split2(p) for p in planes]
    hi = cat([h for h, _ in parts], 1)
    return cat([hi, cat([l for _, l in parts], 1), hi], 0)


def hot_rows(row, n):
    return jnp.where(row == lax.broadcasted_iota(jnp.int32, (n, row.shape[1]), 0), 1.0, 0.0).astype(BF)


def y_forward(yf, planes, a_ref, slab):
    out = dot(yf, stack2(planes))
    out = out[:2 * M] + out[2 * M:]
    for i, o in enumerate(lanes(out, len(planes))):
        a_ref[pl.ds(slab + i, M, stride=A_STRIDE), :] = o[:M]
        a_ref[pl.ds(slab + i + 64, M, stride=A_STRIDE), :] = o[M:]


def z_forward(zf, planes):
    out = dot(zf, stack2(planes))
    first = out[:64] + out[64:128]
    second = out[128:192] + out[192:]
    low = lane_lo((M, G))
    res = []
    for o0, o1 in zip(lanes(first, len(planes)), lanes(second, len(planes))):
        res.append(jnp.where(low, o0[:M], o1[M:]) + swap(jnp.where(low, o0[M:], o1[:M])))
    return res


def x_forward(xf, planes):
    out = dot(xf, stack2(planes))
    out = out[:64] + out[64:]
    low = lane_lo((M, G))
    res = []
    for o in lanes(out, len(planes)):
        rot = swap(o[M:])
        res.append(o[:M] + jnp.where(low, rot, -rot))
    return res


def rotated(modes):
    rot = swap(modes)
    return cat([modes, jnp.where(lane_lo(modes.shape), -rot, rot)], 0)


def mode_inverse(table, modes):
    return lanes(dot(table, stack3([rotated(m) for m in modes])), len(modes))


def z_inverse(zi, modes, iz_ref, ky):
    low = lane_lo((64, G))
    for i, o in enumerate(mode_inverse(zi, modes)):
        o0, o1 = o[:64], o[64:]
        iz_ref[pl.ds(ky + i, 64, stride=IZ_STRIDE), :] = jnp.where(low, o0, swap(o1))
        iz_ref[pl.ds(ky + i + M, 64, stride=IZ_STRIDE), :] = jnp.where(low, swap(o0), o1)


def gelu(v):
    k = 0.7978845608028654
    return 0.5 * v * (1.0 + jnp.tanh(k * (v + 0.044715 * (v * v * v))))


def y_inverse_act(yi, skip2, rows, planes):
    spectral = lanes(dot(yi, stack3(rows)), len(planes))
    parts = [split2(p) for p in planes]
    skipped = dot(cat([cat([h, l], 1) for h, l in parts], 0), skip2)
    return [gelu(spectral[i] + skipped[i * G:(i + 1) * G]) for i in range(len(planes))]


def message_pair(px_ref, feats_ref, b2):
    cells = lax.broadcasted_iota(jnp.int32, (G, G), 0).astype(F32)
    out = []
    for b1 in range(2):
        off = px_ref[pl.ds(b1 * 16 + b2, 1), :] * float(G) - cells
        k = jnp.exp(-off * off / (2.0 * 0.5 * 0.5)).astype(BF)
        out.append(dot(k, feats_ref[b1 * 16 + b2]))
    return cat(out, 1)


def slot_codes(dev, line):
    lane = lax.broadcasted_iota(jnp.int32, (32, G), 1)
    blocks = lax.broadcasted_iota(jnp.int32, (32, G), 0) * G
    none = 32 * G
    rows = []
    for p in range(2):
        owner = (lane & 63) * 2 + p
        first = jnp.full((32, G), none, jnp.int32)
        last = jnp.full((32, G), -1, jnp.int32)
        for t in range(4):
            hit = dev[:, t:t + 1] == owner
            code = blocks + line[:, t:t + 1]
            first = jnp.minimum(first, jnp.where(hit, code, none))
            last = jnp.maximum(last, jnp.where(hit, code, -1))
        first = jnp.min(first, axis=0, keepdims=True)
        last = jnp.max(last, axis=0, keepdims=True)
        second = jnp.where(last == first, -1, last)
        first = jnp.where(first == none, -1, first)
        rows.append(jnp.where(lane[:1] < 64, first, second))
    return cat(rows, 0)


def source_hot(codes):
    block = lax.shift_right_arithmetic(codes, 7)
    return cat([hot_rows(block[0:1], 32), hot_rows(block[1:2], 32)], 0)


def expand(msg, codes):
    low = lane_lo((16, G))
    zero = jnp.zeros((16, G), F32)
    m = msg.astype(F32)
    w = swap(m)
    both = cat([jnp.where(low, m, zero), jnp.where(low, w, zero), jnp.where(low, zero, w), jnp.where(low, zero, m)], 0)
    return tdot(source_hot(codes), both.astype(BF))


def block_sum(codes, rows):
    low = lane_lo((16, G))
    o = dot(source_hot(codes), rows.astype(BF))
    return (jnp.where(low, o[:16], o[48:]) + swap(jnp.where(low, o[16:32], o[32:48]))).astype(BF)


def slab_hot(lt_ref, slab):
    return cat([hot_rows(cat([lt_ref[p, slab], lt_ref[p, 64 + slab]], 1), G) for p in range(2)], 0)


def scatter_plane(lt_ref, rows_ref, slab):
    low = lane_lo((64, G))
    out = dot(slab_hot(lt_ref, slab), rows_ref[pl.ds(slab, 256, stride=ROWS_STRIDE), :].astype(BF))
    return cat([jnp.where(low, out[:64], swap(out[64:128])), jnp.where(low, swap(out[128:192]), out[192:])], 0)


def gather_plane(lt_ref, plane, slab):
    low = lane_lo((64, G))
    zero = jnp.zeros((64, G), F32)
    a, b = plane[:64], plane[64:]
    rhs = cat([jnp.where(low, a, zero), jnp.where(low, swap(a), zero), jnp.where(low, zero, swap(b)), jnp.where(low, zero, b)], 0)
    return tdot(slab_hot(lt_ref, slab), rhs.astype(BF))


def mode_product(f8s, w_ref, kz):
    low = lane_lo((8, G))
    row = lax.rem(lax.broadcasted_iota(jnp.int32, (32, G), 0), 8)
    res = []
    for t, f8 in enumerate(f8s):
        a = jnp.where(low, f8, -f8)
        b = swap(f8)
        ah, bh = a.astype(BF).astype(F32), b.astype(BF).astype(F32)
        lhs = cat([ah, a - ah, bh, b - bh], 0)
        acc = None
        for j in range(0, 8, 2):
            left = cat([jnp.where(row == j, lhs, 0.0).astype(BF), jnp.where(row == j + 1, lhs, 0.0).astype(BF)], 1)
            o = dot(left, cat([w_ref[j, kz + t], w_ref[j + 1, kz + t]], 0))
            acc = o if acc is None else acc + o
        res.append(cat([acc[0:8] + acc[8:16], acc[16:24] + acc[24:32]], 1))
    return res


U = 8


def net_kernel(px_ref, feats_ref, dev_ref, line_ref, w_hbm, skip_ref, yf_ref, zf_ref, xf_ref, xi_ref, zi_ref, yi_ref, out_ref,
               msg32_ref, msg_ref, recv_ref, my_codes_ref, codes_ref, send_ref, rx_ref, back_ref, sums_ref, gs_ref, gr_ref, hs_ref, hr_ref,
               w_ref, skip2_ref, lt_ref, rows_ref, field_ref, a_ref, iz_ref,
               send_sems, recv_sems, local_sems, group_send, group_recv, w_sems):
    slab = lax.axis_index("slab")
    pencil = lax.axis_index("pencil")
    me = slab * 2 + pencil
    mine = lax.div(me, 32)
    inner = lax.rem(me, 32)
    q = lax.rem(slab, 2) * 2 + pencil
    base = slab - lax.rem(slab, 2)

    def coords(d):
        return lax.div(d, 2), lax.rem(d, 2)

    barrier = pltpu.get_barrier_semaphore()

    def greet(i, _):
        pl.semaphore_signal(barrier, inc=1, device_id=coords(lax.rem(me + i, NDEV)), device_id_type=MESH)
        return 0
    lax.fori_loop(1, NDEV, greet, 0)
    loads = [pltpu.make_async_copy(w_hbm.at[l], w_ref.at[l], w_sems.at[l]) for l in range(2)]
    for load in loads:
        load.start()

    my_codes_ref[...] = slot_codes(dev_ref[...], line_ref[...])
    for l in range(2):
        w = skip_ref[l].astype(F32)
        zero = jnp.zeros((C, C), F32)
        block = cat([cat([w, zero], 1), cat([zero, w], 1)], 0).astype(BF)
        skip2_ref[l, :G, :] = block
        skip2_ref[l, G:, :] = block

    def make_messages(i, _):
        outs = [message_pair(px_ref, feats_ref, i * 4 + u) for u in range(4)]
        for u in range(4):
            msg32_ref[pl.ds(i * 4 + u, G, stride=MSG_STRIDE), :] = outs[u]
        return 0
    lax.fori_loop(0, 4, make_messages, 0)

    def pack_messages(i, _):
        for u in range(16):
            x = i * 16 + u
            msg_ref[x] = msg32_ref[pl.ds(pl.multiple_of(x * MSG_STRIDE, 8), 16), :].astype(BF)
        return 0
    lax.fori_loop(0, 8, pack_messages, 0)
    pl.semaphore_wait(barrier, NDEV - 1)

    def chunk(src, d):
        return src.at[d] if src.shape[0] == NDEV else src

    def local(src, dst, st):
        return pltpu.make_async_copy(chunk(src, me), dst.at[me], local_sems.at[st])

    def send_group(src, dst, st, t):
        group = lax.rem(mine + t, 4) * 32
        if t == 0:
            local(src, dst, st).start()

        def one(i, _):
            d = group + lax.rem(inner + i, 32)
            pltpu.make_async_remote_copy(chunk(src, d), dst.at[me], send_sems.at[st], recv_sems.at[st, t],
                                         device_id=coords(d), device_id_type=MESH).start()
            return 0
        lax.fori_loop(1 if t == 0 else 0, 32, one, 0)

    def wait_group(src, dst, st, t):
        if t == 0:
            local(src, dst, st).wait()
        part = dst.at[pl.ds(0, 31 if t == 0 else 32)]
        pltpu.make_async_copy(part, part, recv_sems.at[st, t]).wait()

    def wait_sends(dst, st):
        part = dst.at[pl.ds(0, NDEV - 1)]
        pltpu.make_async_copy(part, part, send_sems.at[st]).wait()

    def peer(i):
        other = lax.rem(q + i, 4)
        return other, (base + lax.div(other, 2), lax.rem(other, 2))

    def send_peer(src, dst, st, i):
        other, did = peer(i)
        return pltpu.make_async_remote_copy(src.at[other], dst.at[q], group_send.at[st, i], group_recv.at[st, i],
                                            device_id=did, device_id_type=MESH)

    def own_part(src, dst, st):
        return pltpu.make_async_copy(src.at[q], dst.at[q], group_recv.at[st, 0])

    for t in range(4):
        send_group(my_codes_ref, codes_ref, 0, t)
    for t in range(4):
        send_group(msg_ref, recv_ref, 1, t)
    for t in range(4):
        wait_group(my_codes_ref, codes_ref, 0, t)
    for p in range(2):
        codes = codes_ref[:, p, :]
        lt_ref[p] = jnp.where(codes >= 0, codes & 127, -1).T.reshape(G, 1, G)

    for t in range(4):
        wait_group(msg_ref, recv_ref, 1, t)
        start = lax.rem(mine + 4 - t, 4) * 32

        def expand_some(i, _):
            s0 = start + i * 16
            outs = [expand(recv_ref[s0 + u], codes_ref[s0 + u]) for u in range(16)]
            for u in range(16):
                for k in range(2):
                    rows_ref[pl.ds(pl.multiple_of((k * G + s0 + u) * ROWS_STRIDE, 8), 64), :] = outs[u][64 * k:64 * k + 64]
            return 0
        lax.fori_loop(0, 2, expand_some, 0)

    def first(g, _):
        s0 = g * U
        planes = [scatter_plane(lt_ref, rows_ref, s0 + i) for i in range(U)]
        for i in range(U):
            field_ref[s0 + i] = planes[i]
        y_forward(yf_ref[...], planes, a_ref, s0)
        return 0
    lax.fori_loop(0, 64 // U, first, 0)
    wait_sends(codes_ref, 0)
    wait_sends(recv_ref, 1)

    for layer in range(2):
        st = 2 + 2 * layer
        rx, back = rx_ref.at[layer], back_ref.at[layer]
        gs, gr, hs, hr = gs_ref, gr_ref.at[layer], hs_ref, hr_ref.at[layer]
        for t in range(4):
            ky = lax.rem(mine + t, 4) * 8
            outs = z_forward(zf_ref[...], [a_ref[pl.ds(pl.multiple_of((ky + i) * A_STRIDE, 8), G), :] for i in range(8)])
            for i in range(8):
                send_ref[pl.ds((ky + i) * 4, 4)] = outs[i].reshape(4, 8, G)
            send_group(send_ref, rx, st, t)
        for t in range(4):
            wait_group(send_ref, rx, st, t)
        rxf = rx.reshape(NDEV * 8, G)
        outs = x_forward(xf_ref[...], [rxf[pl.ds(kz, G, stride=8), :] for kz in range(8)])
        for kz in range(8):
            gs[:, kz] = outs[kz].reshape(4, 8, G)
        own_part(gs, gr, 2 * layer).start()
        for i in range(1, 4):
            send_peer(gs, gr, 2 * layer, i).start()
        loads[layer].wait()
        for i in range(4):
            g = lax.rem(q + i, 4)
            if i == 0:
                own_part(gs, gr, 2 * layer).wait()
            else:
                send_peer(gs, gr, 2 * layer, 4 - i).wait_recv()
            outs = mode_product([gr[g, k] for k in range(8)], w_ref.at[layer], g * 8)
            for k in range(8):
                hs[g, k] = outs[k]
            if i == 0:
                own_part(hs, hr, 2 * layer + 1).start()
            else:
                send_peer(hs, hr, 2 * layer + 1, i).start()
        wait_sends(rx, st)
        own_part(hs, hr, 2 * layer + 1).wait()
        for i in range(1, 4):
            send_peer(hs, hr, 2 * layer + 1, i).wait_recv()
        outs = mode_inverse(xi_ref[...], [hr[:, kz].reshape(M, G) for kz in range(8)])
        for kz in range(8):
            send_ref.reshape(NDEV * 8, G)[pl.ds(kz, G, stride=8), :] = outs[kz]
        for t in range(4):
            send_group(send_ref, back, st + 1, t)
        for i in range(1, 4):
            send_peer(gs, gr, 2 * layer, i).wait_send()
            send_peer(hs, hr, 2 * layer + 1, i).wait_send()
        for t in range(4):
            wait_group(send_ref, back, st + 1, t)
            ky = lax.rem(mine + 4 - t, 4) * 8
            z_inverse(zi_ref[...], [back[pl.ds((ky + i) * 4, 4)].reshape(M, G) for i in range(8)], iz_ref, ky)
        wait_sends(back, st + 1)

        def activate(s0):
            rows = [iz_ref[pl.ds(pl.multiple_of((s0 + i) * IZ_STRIDE, 8), 64), :] for i in range(U)]
            return y_inverse_act(yi_ref[...], skip2_ref[layer], rows, [field_ref[s0 + i] for i in range(U)])

        if layer == 0:
            def middle(g, _):
                planes = activate(g * U)
                for i in range(U):
                    field_ref[g * U + i] = planes[i]
                y_forward(yf_ref[...], planes, a_ref, g * U)
                return 0
            lax.fori_loop(0, 64 // U, middle, 0)
        else:
            def final(g, _):
                planes = activate(g * U)
                outs = [gather_plane(lt_ref, planes[i], g * U + i) for i in range(U)]
                for i in range(U):
                    rows_ref[pl.ds(g * U + i, 256, stride=ROWS_STRIDE), :] = outs[i]
                return 0
            lax.fori_loop(0, 64 // U, final, 0)

    for t in range(4):
        start = lax.rem(mine + t, 4) * 32

        def sum_some(i, _):
            s0 = start + i * 16
            outs = []
            for u in range(16):
                rows = [rows_ref[pl.ds(pl.multiple_of((k * G + s0 + u) * ROWS_STRIDE, 8), 64), :] for k in range(2)]
                outs.append(block_sum(codes_ref[s0 + u], cat(rows, 0)))
            for u in range(16):
                sums_ref[s0 + u] = outs[u]
            return 0
        lax.fori_loop(0, 2, sum_some, 0)
        send_group(sums_ref, out_ref, 6, t)
    for t in range(4):
        wait_group(sums_ref, out_ref, 6, t)
    wait_sends(out_ref, 6)


def kernel_rows(coords):
    offset_x = coords[..., None] * G - jnp.arange(G, dtype=F32)
    return jnp.exp(-offset_x * offset_x / (2.0 * 0.5 * 0.5)).astype(BF)


def per_device(point_feats, point_x, neighbour_dev, neighbour_line, spec_weight, skip_weight):
    tables = [jnp.asarray(t) for t in make_tables()]
    nb = neighbour_dev.shape[0]
    px = point_x.reshape(nb, G)
    feats = point_feats.reshape(nb, G, C)
    weights = spec_weight.reshape(2, 8, M, 2 * C, C)
    vm = pl.BlockSpec(memory_space=pltpu.VMEM)
    chunks = pltpu.VMEM((NDEV, 16, G), BF)
    modes = pltpu.VMEM((NDEV, 8, G), F32)
    pair = pltpu.VMEM((2, NDEV, 8, G), F32)
    group = pltpu.VMEM((4, 8, 8, G), F32)
    group2 = pltpu.VMEM((2, 4, 8, 8, G), F32)
    dma = pltpu.SemaphoreType.DMA
    values = pl.pallas_call(
        net_kernel,
        out_shape=jax.ShapeDtypeStruct((NDEV, 16, G), BF),
        in_specs=[vm] * 4 + [pl.BlockSpec(memory_space=pl.ANY)] + [vm] * 7,
        out_specs=vm,
        scratch_shapes=[
            pltpu.VMEM((G * MSG_STRIDE, G), F32), chunks, chunks, pltpu.VMEM((2, G), jnp.int32), pltpu.VMEM((NDEV, 2, G), jnp.int32),
            modes, pair, pair, chunks, group, group2, group, group2,
            pltpu.VMEM((2, 8, M, 2 * C, C), BF), pltpu.VMEM((2, 2 * G, G), BF), pltpu.VMEM((2, G, 1, G), jnp.int32),
            pltpu.VMEM((256 * ROWS_STRIDE, G), F32), pltpu.VMEM((64, G, G), F32),
            pltpu.VMEM((M * A_STRIDE, G), F32), pltpu.VMEM((64 * IZ_STRIDE, G), F32),
            dma((7,)), dma((7, 4)), dma((7,)), dma((4, 4)), dma((4, 4)), dma((2,)),
        ],
        compiler_params=pltpu.CompilerParams(vmem_limit_bytes=VLIM, collective_id=1, has_side_effects=True),
        name="net",
    )(px, feats, neighbour_dev, neighbour_line, weights, skip_weight, *tables)
    values = values.reshape(G, 16, 2, C).transpose(2, 1, 0, 3).reshape(nb, G, C)
    out = 0.5 * jnp.einsum("bpx,bxc->bpc", kernel_rows(px), values, preferred_element_type=F32)
    return out.reshape(-1, C)


def solution(mesh):
    both = ("slab", "pencil")
    in_specs = (P(both, None), P(both), P(both, None), P(both, None), P(None, both, None, None, None, None), P())
    return jax.shard_map(per_device, mesh=mesh, in_specs=in_specs, out_specs=P(both, None), check_vma=False)
```

```python
import jax
import jax.numpy as jnp
import numpy as np
from jax import lax
from jax.experimental import pallas as pl
from jax.experimental.pallas import tpu as pltpu
from jax.sharding import PartitionSpec as P

G = 128
C = 64
M = 32
NDEV = 128
MESH = pl.DeviceIdType.MESH
BF = jnp.bfloat16
F32 = jnp.float32
VLIM = 60 * 1024 * 1024


def trig(cells):
    waves = np.arange(M) - M // 2
    ang = ((cells[:, None] * waves[None, :]) % G) * (2.0 * np.pi / G)
    return np.cos(ang), np.sin(ang)


def split_np(t):
    hi = np.asarray(t, np.float32).astype(jnp.bfloat16)
    lo = (np.asarray(t, np.float64) - hi.astype(np.float64)).astype(np.float32).astype(jnp.bfloat16)
    return hi, lo


def tall(t):
    hi, lo = split_np(t)
    return np.concatenate([np.concatenate([hi, hi], 1), np.concatenate([lo, np.zeros_like(lo)], 1)], 0)


def wide(t):
    hi, lo = split_np(t)
    return np.concatenate([hi, hi, lo], 1)


def make_tables():
    cos, sin = trig(np.arange(G))
    yf = tall(np.concatenate([cos.T, -sin.T], 0))
    zf = []
    for z1 in range(2):
        c, s = trig(2 * np.arange(G // 2) + z1)
        zf.append(tall(np.concatenate([np.concatenate([c.T, s.T], 1), np.concatenate([-s.T, c.T], 1)], 0)))
    zf = np.concatenate(zf, 0)
    xf = tall(np.concatenate([cos.T, sin.T], 0))
    xi = wide(np.concatenate([cos, sin], 1) / float(G) ** 3)
    zi = wide(np.concatenate([np.concatenate(trig(2 * np.arange(G // 2) + z1), 1) for z1 in range(2)], 0))
    yi = wide(np.concatenate([cos, -sin], 1))
    return yf, zf, xf, xi, zi, yi


ROWS_STRIDE = 72
A_STRIDE = 136
IZ_STRIDE = 72
MSG_STRIDE = 24
cat = jnp.concatenate


def split2(v):
    hi = v.astype(BF)
    return hi, (v - hi.astype(F32)).astype(BF)


def dot(a, b):
    return jnp.dot(a, b, preferred_element_type=F32)


def tdot(a, b):
    return lax.dot_general(a, b, (((0,), (0,)), ((), ())), preferred_element_type=F32)


def lane_lo(shape):
    return lax.broadcasted_iota(jnp.int32, shape, 1) < C


def swap(v):
    return pltpu.roll(v, C, 1)


def lanes(v, n):
    return [v[:, i * G:(i + 1) * G] for i in range(n)]


def stack2(planes):
    parts = [split2(p) for p in planes]
    return cat([cat([h for h, _ in parts], 1), cat([l for _, l in parts], 1)], 0)


def stack3(planes):
    parts = [split2(p) for p in planes]
    hi = cat([h for h, _ in parts], 1)
    return cat([hi, cat([l for _, l in parts], 1), hi], 0)


def hot_rows(row, n):
    return jnp.where(row == lax.broadcasted_iota(jnp.int32, (n, row.shape[1]), 0), 1.0, 0.0).astype(BF)


def y_forward(yf, planes, a_ref, slab):
    out = dot(yf, stack2(planes))
    out = out[:2 * M] + out[2 * M:]
    for i, o in enumerate(lanes(out, len(planes))):
        a_ref[pl.ds(slab + i, M, stride=A_STRIDE), :] = o[:M]
        a_ref[pl.ds(slab + i + 64, M, stride=A_STRIDE), :] = o[M:]


def z_forward(zf, planes):
    out = dot(zf, stack2(planes))
    first = out[:64] + out[64:128]
    second = out[128:192] + out[192:]
    low = lane_lo((M, G))
    res = []
    for o0, o1 in zip(lanes(first, len(planes)), lanes(second, len(planes))):
        res.append(jnp.where(low, o0[:M], o1[M:]) + swap(jnp.where(low, o0[M:], o1[:M])))
    return res


def x_forward(xf, planes):
    out = dot(xf, stack2(planes))
    out = out[:64] + out[64:]
    low = lane_lo((M, G))
    res = []
    for o in lanes(out, len(planes)):
        rot = swap(o[M:])
        res.append(o[:M] + jnp.where(low, rot, -rot))
    return res


def rotated(modes):
    rot = swap(modes)
    return cat([modes, jnp.where(lane_lo(modes.shape), -rot, rot)], 0)


def mode_inverse(table, modes):
    return lanes(dot(table, stack3([rotated(m) for m in modes])), len(modes))


def z_inverse(zi, modes, iz_ref, kys):
    low = lane_lo((64, G))
    for ky, o in zip(kys, mode_inverse(zi, modes)):
        o0, o1 = o[:64], o[64:]
        iz_ref[pl.ds(ky, 64, stride=IZ_STRIDE), :] = jnp.where(low, o0, swap(o1))
        iz_ref[pl.ds(ky + M, 64, stride=IZ_STRIDE), :] = jnp.where(low, swap(o0), o1)


def gelu(v):
    k = 0.7978845608028654
    return 0.5 * v * (1.0 + jnp.tanh(k * (v + 0.044715 * (v * v * v))))


def y_inverse_act(yi, skip2, rows, planes):
    spectral = lanes(dot(yi, stack3(rows)), len(planes))
    parts = [split2(p) for p in planes]
    skipped = dot(cat([cat([h, l], 1) for h, l in parts], 0), skip2)
    return [gelu(spectral[i] + skipped[i * G:(i + 1) * G]) for i in range(len(planes))]


def message_pair(px_ref, feats_ref, b2):
    cells = lax.broadcasted_iota(jnp.int32, (G, G), 0).astype(F32)
    out = []
    for b1 in range(2):
        off = px_ref[pl.ds(b1 * 16 + b2, 1), :] * float(G) - cells
        k = jnp.exp(-off * off / (2.0 * 0.5 * 0.5)).astype(BF)
        feats = feats_ref[:, pl.ds(pl.multiple_of((b1 * 16 + b2) * G, G), G)]
        out.append(lax.dot_general(k, feats, (((1,), (1,)), ((), ())), preferred_element_type=F32))
    return cat(out, 1)


def slot_codes(dev, line):
    lane = lax.broadcasted_iota(jnp.int32, (32, G), 1)
    blocks = lax.broadcasted_iota(jnp.int32, (32, G), 0) * G
    none = 32 * G
    rows = []
    for p in range(2):
        owner = (lane & 63) * 2 + p
        first = jnp.full((32, G), none, jnp.int32)
        last = jnp.full((32, G), -1, jnp.int32)
        for t in range(4):
            hit = dev[:, t:t + 1] == owner
            code = blocks + line[:, t:t + 1]
            first = jnp.minimum(first, jnp.where(hit, code, none))
            last = jnp.maximum(last, jnp.where(hit, code, -1))
        first = jnp.min(first, axis=0, keepdims=True)
        last = jnp.max(last, axis=0, keepdims=True)
        second = jnp.where(last == first, -1, last)
        first = jnp.where(first == none, -1, first)
        rows.append(jnp.where(lane[:1] < 64, first, second))
    return cat(rows, 0)


def source_hot(codes):
    block = lax.shift_right_arithmetic(codes, 7)
    return cat([hot_rows(block[0:1], 32), hot_rows(block[1:2], 32)], 0)


def expand(msg, codes):
    low = lane_lo((16, G))
    zero = jnp.zeros((16, G), F32)
    m = msg.astype(F32)
    w = swap(m)
    both = cat([jnp.where(low, m, zero), jnp.where(low, w, zero), jnp.where(low, zero, w), jnp.where(low, zero, m)], 0)
    return tdot(source_hot(codes), both.astype(BF))


def block_sum(codes, rows):
    low = lane_lo((16, G))
    o = dot(source_hot(codes), rows.astype(BF))
    return (jnp.where(low, o[:16], o[48:]) + swap(jnp.where(low, o[16:32], o[32:48]))).astype(BF)


def slab_hot(lt_ref, slab):
    return cat([hot_rows(cat([lt_ref[p, slab], lt_ref[p, 64 + slab]], 1), G) for p in range(2)], 0)


def scatter_plane(lt_ref, rows_ref, slab):
    low = lane_lo((64, G))
    out = dot(slab_hot(lt_ref, slab), rows_ref[pl.ds(slab, 256, stride=ROWS_STRIDE), :].astype(BF))
    return cat([jnp.where(low, out[:64], swap(out[64:128])), jnp.where(low, swap(out[128:192]), out[192:])], 0)


def gather_plane(lt_ref, plane, slab):
    low = lane_lo((64, G))
    zero = jnp.zeros((64, G), F32)
    a, b = plane[:64], plane[64:]
    rhs = cat([jnp.where(low, a, zero), jnp.where(low, swap(a), zero), jnp.where(low, zero, swap(b)), jnp.where(low, zero, b)], 0)
    return tdot(slab_hot(lt_ref, slab), rhs.astype(BF))


def mode_product(f8s, w_ref, kz):
    low = lane_lo((8, G))
    row = lax.rem(lax.broadcasted_iota(jnp.int32, (32, G), 0), 8)
    res = []
    for t, f8 in enumerate(f8s):
        a = jnp.where(low, f8, -f8)
        b = swap(f8)
        ah, bh = a.astype(BF).astype(F32), b.astype(BF).astype(F32)
        lhs = cat([ah, a - ah, bh, b - bh], 0)
        acc = None
        for j in range(0, 8, 2):
            left = cat([jnp.where(row == j, lhs, 0.0).astype(BF), jnp.where(row == j + 1, lhs, 0.0).astype(BF)], 1)
            o = dot(left, cat([w_ref[j, kz + t], w_ref[j + 1, kz + t]], 0))
            acc = o if acc is None else acc + o
        res.append(cat([acc[0:8] + acc[8:16], acc[16:24] + acc[24:32]], 1))
    return res


U = 8


def net_kernel(px_ref, feats_ref, dev_ref, line_ref, w_hbm, skip_ref, yf_ref, zf_ref, xf_ref, xi_ref, zi_ref, yi_ref, out_ref,
               msg32_ref, msg_ref, recv_ref, my_codes_ref, codes_ref, send_ref, rx_ref, back_ref, stage_ref, sums_ref, gs_ref, gr_ref, hs_ref, hr_ref,
               turn_ref, w_ref, skip2_ref, lt_ref, rows_ref, field_ref, a_ref, iz_ref,
               send_sems, recv_sems, local_sems, group_send, group_recv, w_sems):
    slab = lax.axis_index("slab")
    pencil = lax.axis_index("pencil")
    me = slab * 2 + pencil
    my_y = lax.div(slab, 16)
    mine = lax.rem(my_y + lax.rem(lax.div(slab, 4), 4), 4)
    inner = my_y * 8 + lax.rem(me, 8)
    q = lax.rem(slab, 2) * 2 + pencil
    base = slab - lax.rem(slab, 2)

    def member_ky(group, i):
        y = lax.div(i, 2) if not isinstance(i, int) else i // 2
        return y * 8 + lax.rem(group + 4 - y, 4) * 2 + i % 2

    def member(group, i):
        y = lax.div(i, 8)
        return y * 32 + lax.rem(group + 4 - y, 4) * 8 + lax.rem(i, 8)

    def coords(d):
        return lax.div(d, 2), lax.rem(d, 2)

    barrier = pltpu.get_barrier_semaphore()

    def greet(i, _):
        pl.semaphore_signal(barrier, inc=1, device_id=coords(lax.rem(me + i, NDEV)), device_id_type=MESH)
        return 0
    lax.fori_loop(1, NDEV, greet, 0)
    loads = [pltpu.make_async_copy(w_hbm.at[l], w_ref.at[l], w_sems.at[l]) for l in range(2)]
    for load in loads:
        load.start()

    turn_ref[...] = jnp.zeros((8, G), jnp.int32)
    turn_ref[0:4, 0:32] = dev_ref[...]
    turn_ref[4:8, 0:32] = line_ref[...]
    named = turn_ref[...].T
    my_codes_ref[...] = slot_codes(named[:32, 0:4], named[:32, 4:8])
    for l in range(2):
        w = skip_ref[l].astype(F32)
        zero = jnp.zeros((C, C), F32)
        block = cat([cat([w, zero], 1), cat([zero, w], 1)], 0).astype(BF)
        skip2_ref[l, :G, :] = block
        skip2_ref[l, G:, :] = block

    def make_messages(i, _):
        outs = [message_pair(px_ref, feats_ref, i * 4 + u) for u in range(4)]
        for u in range(4):
            msg32_ref[pl.ds(i * 4 + u, G, stride=MSG_STRIDE), :] = outs[u]
        return 0
    lax.fori_loop(0, 4, make_messages, 0)

    def pack_messages(i, _):
        for u in range(16):
            x = i * 16 + u
            msg_ref[x] = msg32_ref[pl.ds(pl.multiple_of(x * MSG_STRIDE, 8), 16), :].astype(BF)
        return 0
    lax.fori_loop(0, 8, pack_messages, 0)
    pl.semaphore_wait(barrier, NDEV - 1)

    def chunk(src, d):
        return src.at[d] if src.shape[0] == NDEV else src

    def local(src, dst, st):
        return pltpu.make_async_copy(chunk(src, me), dst.at[me], local_sems.at[st])

    def send_group(src, dst, st, t):
        group = lax.rem(mine + t, 4)
        if t == 0:
            local(src, dst, st).start()

        def one(i, _):
            d = member(group, lax.rem(inner + i, 32))
            pltpu.make_async_remote_copy(chunk(src, d), dst.at[me], send_sems.at[st], recv_sems.at[st, t],
                                         device_id=coords(d), device_id_type=MESH).start()
            return 0
        lax.fori_loop(1 if t == 0 else 0, 32, one, 0)

    def wait_group(src, dst, st, t):
        if t == 0:
            local(src, dst, st).wait()
        part = dst.at[pl.ds(0, 31 if t == 0 else 32)]
        pltpu.make_async_copy(part, part, recv_sems.at[st, t]).wait()

    def wait_sends(dst, st):
        part = dst.at[pl.ds(0, NDEV - 1)]
        pltpu.make_async_copy(part, part, send_sems.at[st]).wait()

    def peer(i):
        other = lax.rem(q + i, 4)
        return other, (base + lax.div(other, 2), lax.rem(other, 2))

    def send_peer(src, dst, st, i):
        other, did = peer(i)
        return pltpu.make_async_remote_copy(src.at[other], dst.at[q], group_send.at[st, i], group_recv.at[st, i],
                                            device_id=did, device_id_type=MESH)

    def own_part(src, dst, st):
        return pltpu.make_async_copy(src.at[q], dst.at[q], group_recv.at[st, 0])

    for t in range(4):
        send_group(my_codes_ref, codes_ref, 0, t)
    for t in range(4):
        send_group(msg_ref, recv_ref, 1, t)
    for t in range(4):
        wait_group(my_codes_ref, codes_ref, 0, t)
    for p in range(2):
        codes = codes_ref[:, p, :]
        lt_ref[p] = jnp.where(codes >= 0, codes & 127, -1).T.reshape(G, 1, G)

    for t in range(4):
        wait_group(msg_ref, recv_ref, 1, t)
        group = lax.rem(mine + 4 - t, 4)

        def expand_some(i, _):
            who = [member(group, i * 16 + u) for u in range(16)]
            outs = [expand(recv_ref[s], codes_ref[s]) for s in who]
            for s, out in zip(who, outs):
                for k in range(2):
                    rows_ref[pl.ds(pl.multiple_of((k * G + s) * ROWS_STRIDE, 8), 64), :] = out[64 * k:64 * k + 64]
            return 0
        lax.fori_loop(0, 2, expand_some, 0)

    def first(g, _):
        s0 = g * U
        planes = [scatter_plane(lt_ref, rows_ref, s0 + i) for i in range(U)]
        for i in range(U):
            field_ref[s0 + i] = planes[i]
        y_forward(yf_ref[...], planes, a_ref, s0)
        return 0
    lax.fori_loop(0, 64 // U, first, 0)
    wait_sends(codes_ref, 0)
    wait_sends(recv_ref, 1)

    for layer in range(2):
        st = 2 + 2 * layer
        rx, back = rx_ref.at[layer], back_ref.at[layer]
        gs, gr, hs, hr = gs_ref, gr_ref.at[layer], hs_ref, hr_ref.at[layer]
        for t in range(4):
            group = lax.rem(mine + t, 4)
            kys = [member_ky(group, i) for i in range(8)]
            outs = z_forward(zf_ref[...], [a_ref[pl.ds(pl.multiple_of(ky * A_STRIDE, 8), G), :] for ky in kys])
            for ky, out in zip(kys, outs):
                send_ref[pl.ds(ky * 4, 4)] = out.astype(BF).reshape(4, 8, G)
            send_group(send_ref, rx, st, t)
        for t in range(4):
            wait_group(send_ref, rx, st, t)
        stage_ref[...] = rx[...].reshape(NDEV * 8, G).astype(F32)
        outs = x_forward(xf_ref[...], [stage_ref[pl.ds(kz, G, stride=8), :] for kz in range(8)])
        for kz in range(8):
            gs[:, kz] = outs[kz].reshape(4, 8, G)
        own_part(gs, gr, 2 * layer).start()
        for i in range(1, 4):
            send_peer(gs, gr, 2 * layer, i).start()
        loads[layer].wait()
        for i in range(4):
            g = lax.rem(q + i, 4)
            if i == 0:
                own_part(gs, gr, 2 * layer).wait()
            else:
                send_peer(gs, gr, 2 * layer, 4 - i).wait_recv()
            outs = mode_product([gr[g, k] for k in range(8)], w_ref.at[layer], g * 8)
            for k in range(8):
                hs[g, k] = outs[k]
            if i == 0:
                own_part(hs, hr, 2 * layer + 1).start()
            else:
                send_peer(hs, hr, 2 * layer + 1, i).start()
        wait_sends(rx, st)
        own_part(hs, hr, 2 * layer + 1).wait()
        for i in range(1, 4):
            send_peer(hs, hr, 2 * layer + 1, i).wait_recv()
        outs = mode_inverse(xi_ref[...], [hr[:, kz].reshape(M, G) for kz in range(8)])
        for kz in range(8):
            stage_ref[pl.ds(kz, G, stride=8), :] = outs[kz]
        send_ref[...] = stage_ref[...].astype(BF).reshape(NDEV, 8, G)
        for t in range(4):
            send_group(send_ref, back, st + 1, t)
        for i in range(1, 4):
            send_peer(gs, gr, 2 * layer, i).wait_send()
            send_peer(hs, hr, 2 * layer + 1, i).wait_send()
        for t in range(4):
            wait_group(send_ref, back, st + 1, t)
            group = lax.rem(mine + 4 - t, 4)
            kys = [member_ky(group, i) for i in range(8)]
            z_inverse(zi_ref[...], [back[pl.ds(ky * 4, 4)].reshape(M, G).astype(F32) for ky in kys], iz_ref, kys)
        wait_sends(back, st + 1)

        def activate(s0):
            rows = [iz_ref[pl.ds(pl.multiple_of((s0 + i) * IZ_STRIDE, 8), 64), :] for i in range(U)]
            return y_inverse_act(yi_ref[...], skip2_ref[layer], rows, [field_ref[s0 + i] for i in range(U)])

        if layer == 0:
            def middle(g, _):
                planes = activate(g * U)
                for i in range(U):
                    field_ref[g * U + i] = planes[i]
                y_forward(yf_ref[...], planes, a_ref, g * U)
                return 0
            lax.fori_loop(0, 64 // U, middle, 0)
        else:
            def final(g, _):
                planes = activate(g * U)
                outs = [gather_plane(lt_ref, planes[i], g * U + i) for i in range(U)]
                for i in range(U):
                    rows_ref[pl.ds(g * U + i, 256, stride=ROWS_STRIDE), :] = outs[i]
                return 0
            lax.fori_loop(0, 64 // U, final, 0)

    for t in range(4):
        group = lax.rem(mine + t, 4)

        def sum_some(i, _):
            who = [member(group, i * 16 + u) for u in range(16)]
            outs = []
            for s in who:
                rows = [rows_ref[pl.ds(pl.multiple_of((k * G + s) * ROWS_STRIDE, 8), 64), :] for k in range(2)]
                outs.append(block_sum(codes_ref[s], cat(rows, 0)))
            for s, out in zip(who, outs):
                sums_ref[s] = out
            return 0
        lax.fori_loop(0, 2, sum_some, 0)
        send_group(sums_ref, out_ref, 6, t)
    for t in range(4):
        wait_group(sums_ref, out_ref, 6, t)
    wait_sends(out_ref, 6)


def kernel_rows(coords):
    offset_x = coords[..., None] * G - jnp.arange(G, dtype=F32)
    return jnp.exp(-offset_x * offset_x / (2.0 * 0.5 * 0.5)).astype(BF)


def per_device(point_feats, point_x, neighbour_dev, neighbour_line, spec_weight, skip_weight):
    tables = [jnp.asarray(t) for t in make_tables()]
    nb = neighbour_dev.shape[0]
    px = point_x.reshape(nb, G)
    weights = spec_weight.reshape(2, 8, M, 2 * C, C)
    vm = pl.BlockSpec(memory_space=pltpu.VMEM)
    chunks = pltpu.VMEM((NDEV, 16, G), BF)
    modes = pltpu.VMEM((NDEV, 8, G), BF)
    pair = pltpu.VMEM((2, NDEV, 8, G), BF)
    group = pltpu.VMEM((4, 8, 8, G), F32)
    group2 = pltpu.VMEM((2, 4, 8, 8, G), F32)
    dma = pltpu.SemaphoreType.DMA
    values = pl.pallas_call(
        net_kernel,
        out_shape=jax.ShapeDtypeStruct((NDEV, 16, G), BF),
        in_specs=[vm] * 4 + [pl.BlockSpec(memory_space=pl.ANY)] + [vm] * 7,
        out_specs=vm,
        scratch_shapes=[
            pltpu.VMEM((G * MSG_STRIDE, G), F32), chunks, chunks, pltpu.VMEM((2, G), jnp.int32), pltpu.VMEM((NDEV, 2, G), jnp.int32),
            modes, pair, pair, pltpu.VMEM((NDEV * 8, G), F32), chunks, group, group2, group, group2,
            pltpu.VMEM((8, G), jnp.int32), pltpu.VMEM((2, 8, M, 2 * C, C), BF), pltpu.VMEM((2, 2 * G, G), BF), pltpu.VMEM((2, G, 1, G), jnp.int32),
            pltpu.VMEM((256 * ROWS_STRIDE, G), F32), pltpu.VMEM((64, G, G), F32),
            pltpu.VMEM((M * A_STRIDE, G), F32), pltpu.VMEM((64 * IZ_STRIDE, G), F32),
            dma((7,)), dma((7, 4)), dma((7,)), dma((4, 4)), dma((4, 4)), dma((2,)),
        ],
        compiler_params=pltpu.CompilerParams(vmem_limit_bytes=VLIM, collective_id=1, has_side_effects=True),
        name="net",
    )(px, point_feats.T, neighbour_dev.T, neighbour_line.T, weights, skip_weight, *tables)
    values = values.reshape(G, 16, 2, C).transpose(2, 1, 0, 3).reshape(nb, G, C)
    out = 0.5 * jnp.einsum("bpx,bxc->bpc", kernel_rows(px), values, preferred_element_type=F32)
    return out.reshape(-1, C)


def solution(mesh):
    both = ("slab", "pencil")
    in_specs = (P(both, None), P(both), P(both, None), P(both, None), P(None, both, None, None, None, None), P())
    return jax.shard_map(per_device, mesh=mesh, in_specs=in_specs, out_specs=P(both, None), check_vma=False)
```

```python
import jax
import jax.numpy as jnp
import numpy as np
from jax import lax
from jax.experimental import pallas as pl
from jax.experimental.pallas import tpu as pltpu
from jax.sharding import PartitionSpec as P

G = 128
C = 64
M = 32
NDEV = 128
MESH = pl.DeviceIdType.MESH
BF = jnp.bfloat16
F32 = jnp.float32
VLIM = 60 * 1024 * 1024


def trig(cells):
    waves = np.arange(M) - M // 2
    ang = ((cells[:, None] * waves[None, :]) % G) * (2.0 * np.pi / G)
    return np.cos(ang), np.sin(ang)


def split_np(t):
    hi = np.asarray(t, np.float32).astype(jnp.bfloat16)
    lo = (np.asarray(t, np.float64) - hi.astype(np.float64)).astype(np.float32).astype(jnp.bfloat16)
    return hi, lo


def tall(t):
    hi, lo = split_np(t)
    return np.concatenate([np.concatenate([hi, hi], 1), np.concatenate([lo, np.zeros_like(lo)], 1)], 0)


def wide(t):
    hi, lo = split_np(t)
    return np.concatenate([hi, hi, lo], 1)


def make_tables():
    cos, sin = trig(np.arange(G))
    yf = tall(np.concatenate([cos.T, -sin.T], 0))
    zf = []
    for z1 in range(2):
        c, s = trig(2 * np.arange(G // 2) + z1)
        zf.append(tall(np.concatenate([np.concatenate([c.T, s.T], 1), np.concatenate([-s.T, c.T], 1)], 0)))
    zf = np.concatenate(zf, 0)
    xf = tall(np.concatenate([cos.T, sin.T], 0))
    xi = wide(np.concatenate([cos, sin], 1) / float(G) ** 3)
    zi = wide(np.concatenate([np.concatenate(trig(2 * np.arange(G // 2) + z1), 1) for z1 in range(2)], 0))
    yi = wide(np.concatenate([cos, -sin], 1))
    return yf, zf, xf, xi, zi, yi


ROWS_STRIDE = 72
A_STRIDE = 136
IZ_STRIDE = 72
MSG_STRIDE = 24
cat = jnp.concatenate


def split2(v):
    hi = v.astype(BF)
    return hi, (v - hi.astype(F32)).astype(BF)


def dot(a, b):
    return jnp.dot(a, b, preferred_element_type=F32)


def tdot(a, b):
    return lax.dot_general(a, b, (((0,), (0,)), ((), ())), preferred_element_type=F32)


def lane_lo(shape):
    return lax.broadcasted_iota(jnp.int32, shape, 1) < C


def swap(v):
    return pltpu.roll(v, C, 1)


def lanes(v, n):
    return [v[:, i * G:(i + 1) * G] for i in range(n)]


def stack2(planes):
    parts = [split2(p) for p in planes]
    return cat([cat([h for h, _ in parts], 1), cat([l for _, l in parts], 1)], 0)


def stack3(planes):
    parts = [split2(p) for p in planes]
    hi = cat([h for h, _ in parts], 1)
    return cat([hi, cat([l for _, l in parts], 1), hi], 0)


def hot_rows(row, n):
    return jnp.where(row == lax.broadcasted_iota(jnp.int32, (n, row.shape[1]), 0), 1.0, 0.0).astype(BF)


def y_forward(yf, planes, a_ref, slab):
    out = dot(yf, stack2(planes))
    out = out[:2 * M] + out[2 * M:]
    for i, o in enumerate(lanes(out, len(planes))):
        a_ref[pl.ds(slab + i, M, stride=A_STRIDE), :] = o[:M]
        a_ref[pl.ds(slab + i + 64, M, stride=A_STRIDE), :] = o[M:]


def z_forward(zf, planes):
    out = dot(zf, stack2(planes))
    first = out[:64] + out[64:128]
    second = out[128:192] + out[192:]
    low = lane_lo((M, G))
    res = []
    for o0, o1 in zip(lanes(first, len(planes)), lanes(second, len(planes))):
        res.append(jnp.where(low, o0[:M], o1[M:]) + swap(jnp.where(low, o0[M:], o1[:M])))
    return res


def x_forward(xf, planes):
    out = dot(xf, stack2(planes))
    out = out[:64] + out[64:]
    low = lane_lo((M, G))
    res = []
    for o in lanes(out, len(planes)):
        rot = swap(o[M:])
        res.append(o[:M] + jnp.where(low, rot, -rot))
    return res


def rotated(modes):
    rot = swap(modes)
    return cat([modes, jnp.where(lane_lo(modes.shape), -rot, rot)], 0)


def mode_inverse(table, modes):
    return lanes(dot(table, stack3([rotated(m) for m in modes])), len(modes))


def z_inverse(zi, modes, iz_ref, kys):
    low = lane_lo((64, G))
    for ky, o in zip(kys, mode_inverse(zi, modes)):
        o0, o1 = o[:64], o[64:]
        iz_ref[pl.ds(ky, 64, stride=IZ_STRIDE), :] = jnp.where(low, o0, swap(o1))
        iz_ref[pl.ds(ky + M, 64, stride=IZ_STRIDE), :] = jnp.where(low, swap(o0), o1)


def gelu(v):
    k = 0.7978845608028654
    return 0.5 * v * (1.0 + jnp.tanh(k * (v + 0.044715 * (v * v * v))))


def skip_map(skip2, planes):
    parts = [split2(p) for p in planes]
    out = dot(cat([cat([h, l], 1) for h, l in parts], 0), skip2)
    return [out[i * G:(i + 1) * G] for i in range(len(planes))]


def y_inverse_act(yi, rows, skipped):
    spectral = lanes(dot(yi, stack3(rows)), len(rows))
    return [gelu(a + b) for a, b in zip(spectral, skipped)]


def message_pair(px_ref, feats_ref, b2):
    cells = lax.broadcasted_iota(jnp.int32, (G, G), 0).astype(F32)
    out = []
    for b1 in range(2):
        off = px_ref[pl.ds(b1 * 16 + b2, 1), :] * float(G) - cells
        k = jnp.exp(-off * off / (2.0 * 0.5 * 0.5)).astype(BF)
        feats = feats_ref[:, pl.ds(pl.multiple_of((b1 * 16 + b2) * G, G), G)]
        out.append(lax.dot_general(k, feats, (((1,), (1,)), ((), ())), preferred_element_type=F32))
    return cat(out, 1)


def slot_codes(dev, line):
    lane = lax.broadcasted_iota(jnp.int32, (32, G), 1)
    blocks = lax.broadcasted_iota(jnp.int32, (32, G), 0) * G
    none = 32 * G
    rows = []
    for p in range(2):
        owner = (lane & 63) * 2 + p
        first = jnp.full((32, G), none, jnp.int32)
        last = jnp.full((32, G), -1, jnp.int32)
        for t in range(4):
            hit = dev[:, t:t + 1] == owner
            code = blocks + line[:, t:t + 1]
            first = jnp.minimum(first, jnp.where(hit, code, none))
            last = jnp.maximum(last, jnp.where(hit, code, -1))
        first = jnp.min(first, axis=0, keepdims=True)
        last = jnp.max(last, axis=0, keepdims=True)
        second = jnp.where(last == first, -1, last)
        first = jnp.where(first == none, -1, first)
        rows.append(jnp.where(lane[:1] < 64, first, second))
    return cat(rows, 0)


def source_hot(blk_ref, s):
    return cat([hot_rows(blk_ref[p, pl.ds(s, 1), :], 32) for p in range(2)], 0)


def expand(msg, blk_ref, s):
    low = lane_lo((16, G))
    zero = jnp.zeros((16, G), F32)
    m = msg.astype(F32)
    w = swap(m)
    both = cat([jnp.where(low, m, zero), jnp.where(low, w, zero), jnp.where(low, zero, w), jnp.where(low, zero, m)], 0)
    return tdot(source_hot(blk_ref, s), both.astype(BF))


def block_sum(rows, blk_ref, s):
    low = lane_lo((16, G))
    o = dot(source_hot(blk_ref, s), rows.astype(BF))
    return (jnp.where(low, o[:16], o[48:]) + swap(jnp.where(low, o[16:32], o[32:48]))).astype(BF)


def slab_hot(lt_ref, slab):
    return cat([hot_rows(cat([lt_ref[p, slab], lt_ref[p, 64 + slab]], 1), G) for p in range(2)], 0)


def scatter_plane(lt_ref, rows_ref, slab):
    low = lane_lo((64, G))
    out = dot(slab_hot(lt_ref, slab), rows_ref[pl.ds(slab, 256, stride=ROWS_STRIDE), :].astype(BF))
    return cat([jnp.where(low, out[:64], swap(out[64:128])), jnp.where(low, swap(out[128:192]), out[192:])], 0)


def gather_plane(lt_ref, plane, slab):
    low = lane_lo((64, G))
    zero = jnp.zeros((64, G), F32)
    a, b = plane[:64], plane[64:]
    rhs = cat([jnp.where(low, a, zero), jnp.where(low, swap(a), zero), jnp.where(low, zero, swap(b)), jnp.where(low, zero, b)], 0)
    return tdot(slab_hot(lt_ref, slab), rhs.astype(BF))


def pack_weights(w_ref, pack_ref):
    def body(kz4, _):
        for j in range(4):
            cols = [cat([w_ref[2 * j, kz4 * 4 + e], w_ref[2 * j + 1, kz4 * 4 + e]], 0) for e in range(4)]
            pack_ref[kz4, j] = cat(cols, 1)
        return 0
    lax.fori_loop(0, 8, body, 0)


def mode_product(f8s, pack_ref, kz4):
    low = lane_lo((8, G))
    row = lax.rem(lax.broadcasted_iota(jnp.int32, (32, G), 0), 8)
    lhs = []
    for f8 in f8s:
        a = jnp.where(low, f8, -f8)
        b = swap(f8)
        ah, bh = a.astype(BF).astype(F32), b.astype(BF).astype(F32)
        lhs.append(cat([ah, a - ah, bh, b - bh], 0))
    res = []
    for n in range(len(f8s) // 4):
        acc = None
        for j in range(4):
            left = [cat([jnp.where(row == 2 * j + e, l, 0.0).astype(BF) for e in range(2)], 1) for l in lhs[4 * n:4 * n + 4]]
            o = dot(cat(left, 0), pack_ref[kz4 + n, j])
            acc = o if acc is None else acc + o
        for e in range(4):
            o = acc[32 * e:32 * e + 32, G * (e // 2):G * (e // 2) + G]
            re, im = o[0:8] + o[8:16], o[16:24] + o[24:32]
            res.append(jnp.where(low, re, swap(im)) if e % 2 == 0 else jnp.where(low, swap(re), im))
    return res


U = 8
OFFSETS = (((2, 2), (1, 2), (2, 1), (3, 2)), ((2, 3), (0, 2), (2, 0), (1, 1)), ((1, 3), (3, 1), (3, 3), (0, 1)), ((0, 3), (1, 0), (3, 0), (0, 0)))
FWD = F32
INV = BF


def net_kernel(px_ref, feats_ref, dev_ref, line_ref, w_hbm, skip_ref, yf_ref, zf_ref, xf_ref, xi_ref, zi_ref, yi_ref, out_ref,
               msg32_ref, msg_ref, recv_ref, my_codes_ref, codes_ref, fsend_ref, isend_ref, rx_ref, back_ref, stage_ref, sums_ref, gs_ref, gr_ref, hs_ref, hr_ref,
               turn_ref, w_ref, pack_ref, skip2_ref, lt_ref, blk_ref, rows_ref, field_ref, a_ref, iz_ref,
               send_sems, recv_sems, local_sems, group_send, group_recv, w_sems):
    slab = lax.axis_index("slab")
    pencil = lax.axis_index("pencil")
    me = slab * 2 + pencil
    my_y, my_x, my_z = lax.div(slab, 16), lax.rem(lax.div(slab, 4), 4), lax.rem(slab, 4)
    q = lax.rem(slab, 2) * 2 + pencil
    base = slab - lax.rem(slab, 2)

    def column(t, i, sign):
        dy, dx = OFFSETS[t][i]
        return (lax.rem(my_y + 4 + sign * dy, 4) * 4 + lax.rem(my_x + 4 + sign * dx, 4)) * 4

    def group_kys(t, sign):
        return [lax.div(column(t, i, sign), 2) + h for i in range(4) for h in range(2)]

    def group_devices(t, sign):
        out = []
        for i in range(4):
            first = column(t, i, sign)
            for dz in (2, 1, 3, 0):
                chip = first + lax.rem(my_z + dz, 4)
                out += [(chip, 1 - pencil), (chip, pencil)]
        return out

    def coords(d):
        return lax.div(d, 2), lax.rem(d, 2)

    barrier = pltpu.get_barrier_semaphore()

    def greet(i):
        pl.semaphore_signal(barrier, inc=1, device_id=coords(lax.rem(me + i, NDEV)), device_id_type=MESH)

    for i in range(1, 4):
        greet(i)
    loads = [pltpu.make_async_copy(w_hbm.at[l], w_ref.at[l], w_sems.at[l]) for l in range(2)]

    def make_messages(i, _):
        for u in range(31):
            greet(4 + i * 31 + u)
        outs = [message_pair(px_ref, feats_ref, i * 4 + u) for u in range(4)]
        for u in range(4):
            msg32_ref[pl.ds(i * 4 + u, G, stride=MSG_STRIDE), :] = outs[u]
        return 0
    lax.fori_loop(0, 4, make_messages, 0)

    def pack_messages(i, _):
        for u in range(16):
            x = i * 16 + u
            msg_ref[x] = msg32_ref[pl.ds(pl.multiple_of(x * MSG_STRIDE, 8), 16), :].astype(BF)
        return 0
    lax.fori_loop(0, 8, pack_messages, 0)
    turn_ref[...] = jnp.zeros((8, G), jnp.int32)
    turn_ref[0:4, 0:32] = dev_ref[...]
    turn_ref[4:8, 0:32] = line_ref[...]
    named = turn_ref[...].T
    my_codes_ref[...] = slot_codes(named[:32, 0:4], named[:32, 4:8])
    pl.semaphore_wait(barrier, NDEV - 1)

    def chunk(src, d):
        return src.at[d] if src.shape[0] == NDEV else src

    def local(src, dst, st):
        return pltpu.make_async_copy(chunk(src, me), dst.at[me], local_sems.at[st])

    def send_group(src, dst, st, t):
        if t == 3:
            local(src, dst, st).start()
        for chip, core in group_devices(t, 1)[:31 if t == 3 else 32]:
            pltpu.make_async_remote_copy(chunk(src, chip * 2 + core), dst.at[me], send_sems.at[st], recv_sems.at[st, t],
                                         device_id=(chip, core), device_id_type=MESH).start()

    def wait_group(src, dst, st, t):
        if t == 3:
            local(src, dst, st).wait()
        part = dst.at[pl.ds(0, 31 if t == 3 else 32)]
        pltpu.make_async_copy(part, part, recv_sems.at[st, t]).wait()

    def wait_sends(dst, st):
        part = dst.at[pl.ds(0, NDEV - 1)]
        pltpu.make_async_copy(part, part, send_sems.at[st]).wait()

    def peer(i):
        other = lax.rem(q + i, 4)
        return other, (base + lax.div(other, 2), lax.rem(other, 2))

    def send_peer(src, dst, st, i):
        other, did = peer(i)
        return pltpu.make_async_remote_copy(src.at[other], dst.at[q], group_send.at[st, i], group_recv.at[st, i],
                                            device_id=did, device_id_type=MESH)

    def own_part(src, dst, st):
        return pltpu.make_async_copy(src.at[q], dst.at[q], group_recv.at[st, 0])

    for t in range(4):
        send_group(my_codes_ref, codes_ref, 0, t)
    for t in range(4):
        send_group(msg_ref, recv_ref, 1, t)
    for l in range(2):
        w = skip_ref[l].astype(F32)
        zero = jnp.zeros((C, C), F32)
        block = cat([cat([w, zero], 1), cat([zero, w], 1)], 0).astype(BF)
        skip2_ref[l, :G, :] = block
        skip2_ref[l, G:, :] = block
    for t in range(4):
        wait_group(my_codes_ref, codes_ref, 0, t)
    for p in range(2):
        codes = codes_ref[:, p, :]
        lt_ref[p] = jnp.where(codes >= 0, codes & 127, -1).T.reshape(G, 1, G)
        blk_ref[p] = lax.shift_right_arithmetic(codes, 7)

    for t in range(4):
        wait_group(msg_ref, recv_ref, 1, t)
        for half in range(2):
            who = [column(t, half * 2 + u // 8, -1) * 2 + u % 8 for u in range(16)]
            outs = [expand(recv_ref[s], blk_ref, s) for s in who]
            for s, out in zip(who, outs):
                for k in range(2):
                    rows_ref[pl.ds(pl.multiple_of((k * G + s) * ROWS_STRIDE, 8), 64), :] = out[64 * k:64 * k + 64]

    loads[0].start()

    def first(g, _):
        s0 = g * U
        planes = [scatter_plane(lt_ref, rows_ref, s0 + i) for i in range(U)]
        for i in range(U):
            field_ref[s0 + i] = planes[i]
        y_forward(yf_ref[...], planes, a_ref, s0)
        return 0
    lax.fori_loop(0, 64 // U, first, 0)
    wait_sends(codes_ref, 0)
    wait_sends(recv_ref, 1)

    for layer in range(2):
        st = 2 + 2 * layer
        rx, back = rx_ref.at[layer], back_ref.at[layer]
        gs, gr, hs, hr = gs_ref, gr_ref.at[layer], hs_ref, hr_ref.at[layer]
        for t in range(4):
            kys = group_kys(t, 1)
            outs = z_forward(zf_ref[...], [a_ref[pl.ds(pl.multiple_of(ky * A_STRIDE, 8), G), :] for ky in kys])
            for ky, out in zip(kys, outs):
                fsend_ref[pl.ds(ky * 4, 4)] = out.astype(FWD).reshape(4, 8, G)
            send_group(fsend_ref, rx, st, t)
        loads[layer].wait()
        pack_weights(w_ref.at[layer], pack_ref)
        for t in range(4):
            wait_group(fsend_ref, rx, st, t)
        if FWD == F32:
            by_x = rx.reshape(NDEV * 8, G)
        else:
            by_x = stage_ref
            by_x[...] = rx[...].reshape(NDEV * 8, G).astype(F32)
        outs = x_forward(xf_ref[...], [by_x[pl.ds(kz, G, stride=8), :] for kz in range(8)])
        for kz in range(8):
            gs[:, kz] = outs[kz].reshape(4, 8, G)
        own_part(gs, gr, 2 * layer).start()
        for i in range(1, 4):
            send_peer(gs, gr, 2 * layer, i).start()
        for i in range(4):
            g = lax.rem(q + i, 4)
            if i == 0:
                own_part(gs, gr, 2 * layer).wait()
            else:
                send_peer(gs, gr, 2 * layer, 4 - i).wait_recv()
            outs = mode_product([gr[g, k] for k in range(8)], pack_ref, g * 2)
            for k in range(8):
                hs[g, k] = outs[k]
            if i == 0:
                own_part(hs, hr, 2 * layer + 1).start()
            else:
                send_peer(hs, hr, 2 * layer + 1, i).start()
        wait_sends(rx, st)
        own_part(hs, hr, 2 * layer + 1).wait()
        for i in range(1, 4):
            send_peer(hs, hr, 2 * layer + 1, i).wait_recv()
        outs = mode_inverse(xi_ref[...], [hr[:, kz].reshape(M, G) for kz in range(8)])
        by_x = isend_ref.reshape(NDEV * 8, G) if INV == F32 else stage_ref
        for kz in range(8):
            by_x[pl.ds(kz, G, stride=8), :] = outs[kz]
        if INV != F32:
            isend_ref[...] = stage_ref[...].astype(INV).reshape(NDEV, 8, G)
        for t in range(4):
            send_group(isend_ref, back, st + 1, t)
        for i in range(1, 4):
            send_peer(gs, gr, 2 * layer, i).wait_send()
            send_peer(hs, hr, 2 * layer + 1, i).wait_send()

        def skip_some(g, _):
            outs = skip_map(skip2_ref[layer], [field_ref[g * U + i] for i in range(U)])
            for i in range(U):
                field_ref[g * U + i] = outs[i]
            return 0
        lax.fori_loop(0, 64 // U, skip_some, 0)
        for t in range(4):
            wait_group(isend_ref, back, st + 1, t)
            kys = group_kys(t, -1)
            z_inverse(zi_ref[...], [back[pl.ds(ky * 4, 4)].reshape(M, G).astype(F32) for ky in kys], iz_ref, kys)
        wait_sends(back, st + 1)

        def activate(s0):
            rows = [iz_ref[pl.ds(pl.multiple_of((s0 + i) * IZ_STRIDE, 8), 64), :] for i in range(U)]
            return y_inverse_act(yi_ref[...], rows, [field_ref[s0 + i] for i in range(U)])

        if layer == 0:
            loads[1].start()

            def middle(g, _):
                planes = activate(g * U)
                for i in range(U):
                    field_ref[g * U + i] = planes[i]
                y_forward(yf_ref[...], planes, a_ref, g * U)
                return 0
            lax.fori_loop(0, 64 // U, middle, 0)
        else:
            def final(g, _):
                planes = activate(g * U)
                outs = [gather_plane(lt_ref, planes[i], g * U + i) for i in range(U)]
                for i in range(U):
                    rows_ref[pl.ds(g * U + i, 256, stride=ROWS_STRIDE), :] = outs[i]
                return 0
            lax.fori_loop(0, 64 // U, final, 0)

    for t in range(4):
        for half in range(2):
            who = [column(t, half * 2 + u // 8, 1) * 2 + u % 8 for u in range(16)]
            outs = []
            for s in who:
                rows = [rows_ref[pl.ds(pl.multiple_of((k * G + s) * ROWS_STRIDE, 8), 64), :] for k in range(2)]
                outs.append(block_sum(cat(rows, 0), blk_ref, s))
            for s, out in zip(who, outs):
                sums_ref[s] = out
        send_group(sums_ref, out_ref, 6, t)
    for t in range(4):
        wait_group(sums_ref, out_ref, 6, t)
    wait_sends(out_ref, 6)


def kernel_rows(coords):
    offset_x = coords[..., None] * G - jnp.arange(G, dtype=F32)
    return jnp.exp(-offset_x * offset_x / (2.0 * 0.5 * 0.5)).astype(BF)


def per_device(point_feats, point_x, neighbour_dev, neighbour_line, spec_weight, skip_weight):
    tables = [jnp.asarray(t) for t in make_tables()]
    nb = neighbour_dev.shape[0]
    px = point_x.reshape(nb, G)
    weights = spec_weight.reshape(2, 8, M, 2 * C, C)
    vm = pl.BlockSpec(memory_space=pltpu.VMEM)
    chunks = pltpu.VMEM((NDEV, 16, G), BF)
    modes = [pltpu.VMEM((NDEV, 8, G), t) for t in (FWD, INV)] + [pltpu.VMEM((2, NDEV, 8, G), t) for t in (FWD, INV)]
    group = pltpu.VMEM((4, 8, 8, G), F32)
    group2 = pltpu.VMEM((2, 4, 8, 8, G), F32)
    dma = pltpu.SemaphoreType.DMA
    values = pl.pallas_call(
        net_kernel,
        out_shape=jax.ShapeDtypeStruct((NDEV, 16, G), BF),
        in_specs=[vm] * 4 + [pl.BlockSpec(memory_space=pl.ANY)] + [vm] * 7,
        out_specs=vm,
        scratch_shapes=[
            pltpu.VMEM((G * MSG_STRIDE, G), F32), chunks, chunks, pltpu.VMEM((2, G), jnp.int32), pltpu.VMEM((NDEV, 2, G), jnp.int32),
            *modes, pltpu.VMEM((NDEV * 8, G), F32), chunks, group, group2, group, group2,
            pltpu.VMEM((8, G), jnp.int32), pltpu.VMEM((2, 8, M, 2 * C, C), BF), pltpu.VMEM((8, 4, 256, 256), BF), pltpu.VMEM((2, 2 * G, G), BF), pltpu.VMEM((2, G, 1, G), jnp.int32), pltpu.VMEM((2, G, G), jnp.int32),
            pltpu.VMEM((256 * ROWS_STRIDE, G), F32), pltpu.VMEM((64, G, G), F32),
            pltpu.VMEM((M * A_STRIDE, G), F32), pltpu.VMEM((64 * IZ_STRIDE, G), F32),
            dma((7,)), dma((7, 4)), dma((7,)), dma((4, 4)), dma((4, 4)), dma((2,)),
        ],
        compiler_params=pltpu.CompilerParams(vmem_limit_bytes=VLIM, collective_id=1, has_side_effects=True),
        name="net",
    )(px, point_feats.T, neighbour_dev.T, neighbour_line.T, weights, skip_weight, *tables)
    values = values.reshape(G, 16, 2, C).transpose(2, 1, 0, 3).reshape(nb, G, C)
    out = 0.5 * jnp.einsum("bpx,bxc->bpc", kernel_rows(px), values, preferred_element_type=F32)
    return out.reshape(-1, C)


def solution(mesh):
    both = ("slab", "pencil")
    in_specs = (P(both, None), P(both), P(both, None), P(both, None), P(None, both, None, None, None, None), P())
    return jax.shard_map(per_device, mesh=mesh, in_specs=in_specs, out_specs=P(both, None), check_vma=False)
```

```python
import jax
import jax.numpy as jnp
import numpy as np
from jax import lax
from jax.experimental import pallas as pl
from jax.experimental.pallas import tpu as pltpu
from jax.sharding import PartitionSpec as P

G = 128
C = 64
M = 32
NDEV = 128
MESH = pl.DeviceIdType.MESH
BF = jnp.bfloat16
F32 = jnp.float32
VLIM = 60 * 1024 * 1024


def trig(cells):
    waves = np.arange(M) - M // 2
    ang = ((cells[:, None] * waves[None, :]) % G) * (2.0 * np.pi / G)
    return np.cos(ang), np.sin(ang)


def split_np(t):
    hi = np.asarray(t, np.float32).astype(jnp.bfloat16)
    lo = (np.asarray(t, np.float64) - hi.astype(np.float64)).astype(np.float32).astype(jnp.bfloat16)
    return hi, lo


def tall(t):
    hi, lo = split_np(t)
    return np.concatenate([np.concatenate([hi, hi], 1), np.concatenate([lo, np.zeros_like(lo)], 1)], 0)


def wide(t):
    hi, lo = split_np(t)
    return np.concatenate([hi, hi, lo], 1)


def make_tables():
    cos, sin = trig(np.arange(G))
    yf = tall(np.concatenate([cos.T, -sin.T], 0))
    zf = []
    for z1 in range(2):
        c, s = trig(2 * np.arange(G // 2) + z1)
        zf.append(tall(np.concatenate([np.concatenate([c.T, s.T], 1), np.concatenate([-s.T, c.T], 1)], 0)))
    zf = np.concatenate(zf, 0)
    xf = tall(np.concatenate([cos.T, sin.T], 0))
    xi = wide(np.concatenate([cos, sin], 1) / float(G) ** 3)
    zi = wide(np.concatenate([np.concatenate(trig(2 * np.arange(G // 2) + z1), 1) for z1 in range(2)], 0))
    yi = wide(np.concatenate([cos, -sin], 1))
    return yf, zf, xf, xi, zi, yi


ROWS_STRIDE = 72
A_STRIDE = 136
IZ_STRIDE = 72
MSG_STRIDE = 24
cat = jnp.concatenate


def split2(v):
    hi = v.astype(BF)
    return hi, (v - hi.astype(F32)).astype(BF)


def dot(a, b):
    return jnp.dot(a, b, preferred_element_type=F32)


def tdot(a, b):
    return lax.dot_general(a, b, (((0,), (0,)), ((), ())), preferred_element_type=F32)


def lane_lo(shape):
    return lax.broadcasted_iota(jnp.int32, shape, 1) < C


def swap(v):
    return pltpu.roll(v, C, 1)


def lanes(v, n):
    return [v[:, i * G:(i + 1) * G] for i in range(n)]


def stack2(planes):
    parts = [split2(p) for p in planes]
    return cat([cat([h for h, _ in parts], 1), cat([l for _, l in parts], 1)], 0)


def stack3(planes):
    parts = [split2(p) for p in planes]
    hi = cat([h for h, _ in parts], 1)
    return cat([hi, cat([l for _, l in parts], 1), hi], 0)


def hot_rows(row, n):
    return jnp.where(row == lax.broadcasted_iota(jnp.int32, (n, row.shape[1]), 0), 1.0, 0.0).astype(BF)


def y_forward(yf, planes, a_ref, slab):
    out = dot(yf, stack2(planes))
    out = out[:2 * M] + out[2 * M:]
    for i, o in enumerate(lanes(out, len(planes))):
        a_ref[pl.ds(slab + i, M, stride=A_STRIDE), :] = o[:M]
        a_ref[pl.ds(slab + i + 64, M, stride=A_STRIDE), :] = o[M:]


def z_forward(zf, planes):
    out = dot(zf, stack2(planes))
    first = out[:64] + out[64:128]
    second = out[128:192] + out[192:]
    low = lane_lo((M, G))
    res = []
    for o0, o1 in zip(lanes(first, len(planes)), lanes(second, len(planes))):
        res.append(jnp.where(low, o0[:M], o1[M:]) + swap(jnp.where(low, o0[M:], o1[:M])))
    return res


def x_forward(xf, planes):
    out = dot(xf, stack2(planes))
    out = out[:64] + out[64:]
    low = lane_lo((M, G))
    res = []
    for o in lanes(out, len(planes)):
        rot = swap(o[M:])
        res.append(o[:M] + jnp.where(low, rot, -rot))
    return res


def rotated(modes):
    rot = swap(modes)
    return cat([modes, jnp.where(lane_lo(modes.shape), -rot, rot)], 0)


def mode_inverse(table, modes):
    return lanes(dot(table, stack3([rotated(m) for m in modes])), len(modes))


def z_inverse(zi, modes, iz_ref, kys):
    low = lane_lo((64, G))
    for ky, o in zip(kys, mode_inverse(zi, modes)):
        o0, o1 = o[:64], o[64:]
        iz_ref[pl.ds(ky, 64, stride=IZ_STRIDE), :] = jnp.where(low, o0, swap(o1))
        iz_ref[pl.ds(ky + M, 64, stride=IZ_STRIDE), :] = jnp.where(low, swap(o0), o1)


def gelu(v):
    k = 0.7978845608028654
    return 0.5 * v * (1.0 + jnp.tanh(k * (v + 0.044715 * (v * v * v))))


def skip_map(skip2, planes):
    parts = [split2(p) for p in planes]
    out = dot(cat([cat([h, l], 1) for h, l in parts], 0), skip2)
    return [out[i * G:(i + 1) * G] for i in range(len(planes))]


def y_inverse_act(yi, rows, skipped):
    spectral = lanes(dot(yi, stack3(rows)), len(rows))
    return [gelu(a + b) for a, b in zip(spectral, skipped)]


def message_pair(px_ref, feats_ref, b2):
    cells = lax.broadcasted_iota(jnp.int32, (G, G), 0).astype(F32)
    out = []
    for b1 in range(2):
        off = px_ref[pl.ds(b1 * 16 + b2, 1), :] * float(G) - cells
        k = jnp.exp(-off * off / (2.0 * 0.5 * 0.5)).astype(BF)
        feats = feats_ref[:, pl.ds(pl.multiple_of((b1 * 16 + b2) * G, G), G)]
        out.append(lax.dot_general(k, feats, (((1,), (1,)), ((), ())), preferred_element_type=F32))
    return cat(out, 1)


def slot_codes(dev, line):
    lane = lax.broadcasted_iota(jnp.int32, (32, G), 1)
    blocks = lax.broadcasted_iota(jnp.int32, (32, G), 0) * G
    none = 32 * G
    rows = []
    for p in range(2):
        owner = (lane & 63) * 2 + p
        first = jnp.full((32, G), none, jnp.int32)
        last = jnp.full((32, G), -1, jnp.int32)
        for t in range(4):
            hit = dev[:, t:t + 1] == owner
            code = blocks + line[:, t:t + 1]
            first = jnp.minimum(first, jnp.where(hit, code, none))
            last = jnp.maximum(last, jnp.where(hit, code, -1))
        first = jnp.min(first, axis=0, keepdims=True)
        last = jnp.max(last, axis=0, keepdims=True)
        second = jnp.where(last == first, -1, last)
        first = jnp.where(first == none, -1, first)
        rows.append(jnp.where(lane[:1] < 64, first, second))
    return cat(rows, 0)


def source_hot(blk_ref, s):
    return cat([hot_rows(blk_ref[p, pl.ds(s, 1), :], 32) for p in range(2)], 0)


def expand(msg, blk_ref, s):
    low = lane_lo((16, G))
    zero = jnp.zeros((16, G), F32)
    m = msg.astype(F32)
    w = swap(m)
    both = cat([jnp.where(low, m, zero), jnp.where(low, w, zero), jnp.where(low, zero, w), jnp.where(low, zero, m)], 0)
    return tdot(source_hot(blk_ref, s), both.astype(BF))


def block_sum(rows, blk_ref, s):
    low = lane_lo((16, G))
    o = dot(source_hot(blk_ref, s), rows.astype(BF))
    return (jnp.where(low, o[:16], o[48:]) + swap(jnp.where(low, o[16:32], o[32:48]))).astype(BF)


def slab_hot(lt_ref, slab):
    return cat([hot_rows(cat([lt_ref[p, slab], lt_ref[p, 64 + slab]], 1), G) for p in range(2)], 0)


def scatter_plane(lt_ref, rows_ref, slab):
    low = lane_lo((64, G))
    out = dot(slab_hot(lt_ref, slab), rows_ref[pl.ds(slab, 256, stride=ROWS_STRIDE), :].astype(BF))
    return cat([jnp.where(low, out[:64], swap(out[64:128])), jnp.where(low, swap(out[128:192]), out[192:])], 0)


def gather_plane(lt_ref, plane, slab):
    low = lane_lo((64, G))
    zero = jnp.zeros((64, G), F32)
    a, b = plane[:64], plane[64:]
    rhs = cat([jnp.where(low, a, zero), jnp.where(low, swap(a), zero), jnp.where(low, zero, swap(b)), jnp.where(low, zero, b)], 0)
    return tdot(slab_hot(lt_ref, slab), rhs.astype(BF))


def pack_weights(w_ref, pack_ref):
    def body(kz4, _):
        for j in range(4):
            cols = [cat([w_ref[2 * j, kz4 * 4 + e], w_ref[2 * j + 1, kz4 * 4 + e]], 0) for e in range(4)]
            pack_ref[kz4, j] = cat(cols, 1)
        return 0
    lax.fori_loop(0, 8, body, 0)


def mode_product(f8s, pack_ref, kz4):
    low = lane_lo((8, G))
    row = lax.rem(lax.broadcasted_iota(jnp.int32, (32, G), 0), 8)
    lhs = []
    for f8 in f8s:
        a = jnp.where(low, f8, -f8)
        b = swap(f8)
        ah, bh = a.astype(BF).astype(F32), b.astype(BF).astype(F32)
        lhs.append(cat([ah, a - ah, bh, b - bh], 0))
    res = []
    for n in range(len(f8s) // 4):
        acc = None
        for j in range(4):
            left = [cat([jnp.where(row == 2 * j + e, l, 0.0).astype(BF) for e in range(2)], 1) for l in lhs[4 * n:4 * n + 4]]
            o = dot(cat(left, 0), pack_ref[kz4 + n, j])
            acc = o if acc is None else acc + o
        for e in range(4):
            o = acc[32 * e:32 * e + 32, G * (e // 2):G * (e // 2) + G]
            re, im = o[0:8] + o[8:16], o[16:24] + o[24:32]
            res.append(jnp.where(low, re, swap(im)) if e % 2 == 0 else jnp.where(low, swap(re), im))
    return res


U = 16
OFFSETS = (((2, 2), (1, 2), (2, 1), (3, 2)), ((2, 3), (0, 2), (2, 0), (1, 1)), ((1, 3), (3, 1), (3, 3), (0, 1)), ((0, 3), (1, 0), (3, 0), (0, 0)))
FWD = F32
INV = BF


def net_kernel(px_ref, feats_ref, dev_ref, line_ref, w_hbm, skip_ref, yf_ref, zf_ref, xf_ref, xi_ref, zi_ref, yi_ref, out_ref,
               msg32_ref, msg_ref, recv_ref, my_codes_ref, codes_ref, fsend_ref, isend_ref, rx_ref, back_ref, stage_ref, sums_ref, gs_ref, gr_ref, hs_ref, hr_ref,
               turn_ref, w_ref, pack_ref, skip2_ref, lt_ref, blk_ref, rows_ref, field_ref, a_ref, iz_ref,
               send_sems, recv_sems, local_sems, group_send, group_recv, w_sems):
    slab = lax.axis_index("slab")
    pencil = lax.axis_index("pencil")
    me = slab * 2 + pencil
    my_y, my_x, my_z = lax.div(slab, 16), lax.rem(lax.div(slab, 4), 4), lax.rem(slab, 4)
    q = lax.rem(slab, 2) * 2 + pencil
    base = slab - lax.rem(slab, 2)

    def column(t, i, sign):
        dy, dx = OFFSETS[t][i]
        return (lax.rem(my_y + 4 + sign * dy, 4) * 4 + lax.rem(my_x + 4 + sign * dx, 4)) * 4

    def group_kys(t, sign):
        return [lax.div(column(t, i, sign), 2) + h for i in range(4) for h in range(2)]

    def group_devices(t, sign):
        out = []
        for i in range(4):
            first = column(t, i, sign)
            for dz in (2, 1, 3, 0):
                chip = first + lax.rem(my_z + dz, 4)
                out += [(chip, 1 - pencil), (chip, pencil)]
        return out

    def coords(d):
        return lax.div(d, 2), lax.rem(d, 2)

    barrier = pltpu.get_barrier_semaphore()

    def greet(i):
        pl.semaphore_signal(barrier, inc=1, device_id=coords(lax.rem(me + i, NDEV)), device_id_type=MESH)

    for i in range(1, 4):
        greet(i)
    loads = [pltpu.make_async_copy(w_hbm.at[l], w_ref.at[l], w_sems.at[l]) for l in range(2)]

    def make_messages(i, _):
        for u in range(31):
            greet(4 + i * 31 + u)
        outs = [message_pair(px_ref, feats_ref, i * 4 + u) for u in range(4)]
        for u in range(4):
            msg32_ref[pl.ds(i * 4 + u, G, stride=MSG_STRIDE), :] = outs[u]
        return 0
    lax.fori_loop(0, 4, make_messages, 0)

    def pack_messages(i, _):
        for u in range(16):
            x = i * 16 + u
            msg_ref[x] = msg32_ref[pl.ds(pl.multiple_of(x * MSG_STRIDE, 8), 16), :].astype(BF)
        return 0
    lax.fori_loop(0, 8, pack_messages, 0)
    turn_ref[...] = jnp.zeros((8, G), jnp.int32)
    turn_ref[0:4, 0:32] = dev_ref[...]
    turn_ref[4:8, 0:32] = line_ref[...]
    named = turn_ref[...].T
    my_codes_ref[...] = slot_codes(named[:32, 0:4], named[:32, 4:8])
    pl.semaphore_wait(barrier, NDEV - 1)

    def chunk(src, d):
        return src.at[d] if src.shape[0] == NDEV else src

    def local(src, dst, st):
        return pltpu.make_async_copy(chunk(src, me), dst.at[me], local_sems.at[st])

    def send_group(src, dst, st, t):
        if t == 3:
            local(src, dst, st).start()
        for chip, core in group_devices(t, 1)[:31 if t == 3 else 32]:
            pltpu.make_async_remote_copy(chunk(src, chip * 2 + core), dst.at[me], send_sems.at[st], recv_sems.at[st, t],
                                         device_id=(chip, core), device_id_type=MESH).start()

    def wait_group(src, dst, st, t):
        if t == 3:
            local(src, dst, st).wait()
        part = dst.at[pl.ds(0, 31 if t == 3 else 32)]
        pltpu.make_async_copy(part, part, recv_sems.at[st, t]).wait()

    def wait_sends(dst, st):
        part = dst.at[pl.ds(0, NDEV - 1)]
        pltpu.make_async_copy(part, part, send_sems.at[st]).wait()

    def peer(i):
        other = lax.rem(q + i, 4)
        return other, (base + lax.div(other, 2), lax.rem(other, 2))

    def send_peer(src, dst, st, i):
        other, did = peer(i)
        return pltpu.make_async_remote_copy(src.at[other], dst.at[q], group_send.at[st, i], group_recv.at[st, i],
                                            device_id=did, device_id_type=MESH)

    def own_part(src, dst, st):
        return pltpu.make_async_copy(src.at[q], dst.at[q], group_recv.at[st, 0])

    for t in range(4):
        send_group(my_codes_ref, codes_ref, 0, t)
    for t in range(4):
        send_group(msg_ref, recv_ref, 1, t)
    for l in range(2):
        w = skip_ref[l].astype(F32)
        zero = jnp.zeros((C, C), F32)
        block = cat([cat([w, zero], 1), cat([zero, w], 1)], 0).astype(BF)
        skip2_ref[l, :G, :] = block
        skip2_ref[l, G:, :] = block
    for t in range(4):
        wait_group(my_codes_ref, codes_ref, 0, t)
    for p in range(2):
        codes = codes_ref[:, p, :]
        lt_ref[p] = jnp.where(codes >= 0, codes & 127, -1).T.reshape(G, 1, G)
        blk_ref[p] = lax.shift_right_arithmetic(codes, 7)

    for t in range(4):
        wait_group(msg_ref, recv_ref, 1, t)
        for half in range(2):
            who = [column(t, half * 2 + u // 8, -1) * 2 + u % 8 for u in range(16)]
            outs = [expand(recv_ref[s], blk_ref, s) for s in who]
            for s, out in zip(who, outs):
                for k in range(2):
                    rows_ref[pl.ds(pl.multiple_of((k * G + s) * ROWS_STRIDE, 8), 64), :] = out[64 * k:64 * k + 64]

    loads[0].start()

    def first(g, _):
        s0 = g * U
        planes = [scatter_plane(lt_ref, rows_ref, s0 + i) for i in range(U)]
        for i in range(U):
            field_ref[s0 + i] = planes[i]
        y_forward(yf_ref[...], planes, a_ref, s0)
        return 0
    lax.fori_loop(0, 64 // U, first, 0)
    wait_sends(codes_ref, 0)
    wait_sends(recv_ref, 1)

    for layer in range(2):
        st = 2 + 2 * layer
        rx, back = rx_ref.at[layer], back_ref.at[layer]
        gs, gr, hs, hr = gs_ref, gr_ref.at[layer], hs_ref, hr_ref.at[layer]
        for t in range(4):
            kys = group_kys(t, 1)
            outs = z_forward(zf_ref[...], [a_ref[pl.ds(pl.multiple_of(ky * A_STRIDE, 8), G), :] for ky in kys])
            for ky, out in zip(kys, outs):
                fsend_ref[pl.ds(ky * 4, 4)] = out.astype(FWD).reshape(4, 8, G)
            send_group(fsend_ref, rx, st, t)
        loads[layer].wait()
        pack_weights(w_ref.at[layer], pack_ref)
        for t in range(4):
            wait_group(fsend_ref, rx, st, t)
        if FWD == F32:
            by_x = rx.reshape(NDEV * 8, G)
        else:
            by_x = stage_ref
            by_x[...] = rx[...].reshape(NDEV * 8, G).astype(F32)
        outs = x_forward(xf_ref[...], [by_x[pl.ds(kz, G, stride=8), :] for kz in range(8)])
        for kz in range(8):
            gs[:, kz] = outs[kz].reshape(4, 8, G)
        own_part(gs, gr, 2 * layer).start()
        for i in range(1, 4):
            send_peer(gs, gr, 2 * layer, i).start()
        for i in range(4):
            g = lax.rem(q + i, 4)
            if i == 0:
                own_part(gs, gr, 2 * layer).wait()
            else:
                send_peer(gs, gr, 2 * layer, 4 - i).wait_recv()
            outs = mode_product([gr[g, k] for k in range(8)], pack_ref, g * 2)
            for k in range(8):
                hs[g, k] = outs[k]
            if i == 0:
                own_part(hs, hr, 2 * layer + 1).start()
            else:
                send_peer(hs, hr, 2 * layer + 1, i).start()
        wait_sends(rx, st)
        own_part(hs, hr, 2 * layer + 1).wait()
        for i in range(1, 4):
            send_peer(hs, hr, 2 * layer + 1, i).wait_recv()
        outs = mode_inverse(xi_ref[...], [hr[:, kz].reshape(M, G) for kz in range(8)])
        by_x = isend_ref.reshape(NDEV * 8, G) if INV == F32 else stage_ref
        for kz in range(8):
            by_x[pl.ds(kz, G, stride=8), :] = outs[kz]
        if INV != F32:
            isend_ref[...] = stage_ref[...].astype(INV).reshape(NDEV, 8, G)
        for t in range(4):
            send_group(isend_ref, back, st + 1, t)
        for i in range(1, 4):
            send_peer(gs, gr, 2 * layer, i).wait_send()
            send_peer(hs, hr, 2 * layer + 1, i).wait_send()

        def skip_some(g, _):
            outs = skip_map(skip2_ref[layer], [field_ref[g * U + i] for i in range(U)])
            for i in range(U):
                field_ref[g * U + i] = outs[i]
            return 0
        lax.fori_loop(0, 64 // U, skip_some, 0)
        for t in range(4):
            wait_group(isend_ref, back, st + 1, t)
            kys = group_kys(t, -1)
            z_inverse(zi_ref[...], [back[pl.ds(ky * 4, 4)].reshape(M, G).astype(F32) for ky in kys], iz_ref, kys)
        wait_sends(back, st + 1)

        def activate(s0):
            rows = [iz_ref[pl.ds(pl.multiple_of((s0 + i) * IZ_STRIDE, 8), 64), :] for i in range(U)]
            return y_inverse_act(yi_ref[...], rows, [field_ref[s0 + i] for i in range(U)])

        if layer == 0:
            loads[1].start()

            def middle(g, _):
                planes = activate(g * U)
                for i in range(U):
                    field_ref[g * U + i] = planes[i]
                y_forward(yf_ref[...], planes, a_ref, g * U)
                return 0
            lax.fori_loop(0, 64 // U, middle, 0)
        else:
            def final(g, _):
                planes = activate(g * U)
                outs = [gather_plane(lt_ref, planes[i], g * U + i) for i in range(U)]
                for i in range(U):
                    rows_ref[pl.ds(g * U + i, 256, stride=ROWS_STRIDE), :] = outs[i]
                return 0
            lax.fori_loop(0, 64 // U, final, 0)

    for t in range(4):
        for half in range(2):
            who = [column(t, half * 2 + u // 8, 1) * 2 + u % 8 for u in range(16)]
            outs = []
            for s in who:
                rows = [rows_ref[pl.ds(pl.multiple_of((k * G + s) * ROWS_STRIDE, 8), 64), :] for k in range(2)]
                outs.append(block_sum(cat(rows, 0), blk_ref, s))
            for s, out in zip(who, outs):
                sums_ref[s] = out
        send_group(sums_ref, out_ref, 6, t)
    for t in range(4):
        wait_group(sums_ref, out_ref, 6, t)
    wait_sends(out_ref, 6)


def kernel_rows(coords):
    offset_x = coords[..., None] * G - jnp.arange(G, dtype=F32)
    return jnp.exp(-offset_x * offset_x / (2.0 * 0.5 * 0.5)).astype(BF)


def per_device(point_feats, point_x, neighbour_dev, neighbour_line, spec_weight, skip_weight):
    tables = [jnp.asarray(t) for t in make_tables()]
    nb = neighbour_dev.shape[0]
    px = point_x.reshape(nb, G)
    weights = spec_weight.reshape(2, 8, M, 2 * C, C)
    vm = pl.BlockSpec(memory_space=pltpu.VMEM)
    chunks = pltpu.VMEM((NDEV, 16, G), BF)
    modes = [pltpu.VMEM((NDEV, 8, G), t) for t in (FWD, INV)] + [pltpu.VMEM((2, NDEV, 8, G), t) for t in (FWD, INV)]
    group = pltpu.VMEM((4, 8, 8, G), F32)
    group2 = pltpu.VMEM((2, 4, 8, 8, G), F32)
    dma = pltpu.SemaphoreType.DMA
    values = pl.pallas_call(
        net_kernel,
        out_shape=jax.ShapeDtypeStruct((NDEV, 16, G), BF),
        in_specs=[vm] * 4 + [pl.BlockSpec(memory_space=pl.ANY)] + [vm] * 7,
        out_specs=vm,
        scratch_shapes=[
            pltpu.VMEM((G * MSG_STRIDE, G), F32), chunks, chunks, pltpu.VMEM((2, G), jnp.int32), pltpu.VMEM((NDEV, 2, G), jnp.int32),
            *modes, pltpu.VMEM((NDEV * 8, G), F32), chunks, group, group2, group, group2,
            pltpu.VMEM((8, G), jnp.int32), pltpu.VMEM((2, 8, M, 2 * C, C), BF), pltpu.VMEM((8, 4, 256, 256), BF), pltpu.VMEM((2, 2 * G, G), BF), pltpu.VMEM((2, G, 1, G), jnp.int32), pltpu.VMEM((2, G, G), jnp.int32),
            pltpu.VMEM((256 * ROWS_STRIDE, G), F32), pltpu.VMEM((64, G, G), F32),
            pltpu.VMEM((M * A_STRIDE, G), F32), pltpu.VMEM((64 * IZ_STRIDE, G), F32),
            dma((7,)), dma((7, 4)), dma((7,)), dma((4, 4)), dma((4, 4)), dma((2,)),
        ],
        compiler_params=pltpu.CompilerParams(vmem_limit_bytes=VLIM, collective_id=1, has_side_effects=True),
        name="net",
    )(px, point_feats.T, neighbour_dev.T, neighbour_line.T, weights, skip_weight, *tables)
    values = values.reshape(G, 16, 2, C).transpose(2, 1, 0, 3).reshape(nb, G, C)
    out = 0.5 * jnp.einsum("bpx,bxc->bpc", kernel_rows(px), values, preferred_element_type=F32)
    return out.reshape(-1, C)


def solution(mesh):
    both = ("slab", "pencil")
    in_specs = (P(both, None), P(both), P(both, None), P(both, None), P(None, both, None, None, None, None), P())
    return jax.shard_map(per_device, mesh=mesh, in_specs=in_specs, out_specs=P(both, None), check_vma=False)
```
